256 devices in a mesh: dp: 4 (over y_hi, core), tm: 8 (over x, y_lo), mp: 8 (over z).
Axes of the slice: x: 4, y: 4 (y_hi: 2, y_lo: 2; y = y_hi * 2 + y_lo), z: 8, core: 2. Of those that a mesh axis runs over, the one named last changes fastest.
Arguments:
- spans: bfloat16 [4, 16, 256, 4096], P('dp', 'tm', None, 'mp'), may hold values from -6 to 6
- frame_span: int32 [4, 8], P('dp', 'tm'), may hold values from 0 to 1
- norm_gain: bfloat16 [4096], P('mp'), may hold values from 0.5 to 6
- w_query: bfloat16 [4096, 2048], P(('dp', 'tm'), 'mp'), may hold values from -0.09375 to 0.09375
- w_key: bfloat16 [4096, 2048], P(('dp', 'tm'), 'mp'), may hold values from -0.09375 to 0.09375
- w_value: bfloat16 [4096, 2048], P(('dp', 'tm'), 'mp'), may hold values from -0.09375 to 0.09375
- w_out: bfloat16 [2048, 4096], P('mp', ('dp', 'tm')), may hold values from -0.125 to 0.125
- grad_out: bfloat16 [4, 8, 256, 4096], P('dp', 'tm', None, 'mp'), may hold values from -6 to 6
Outputs:
- span_grad: bfloat16 [4, 16, 256, 4096], P('dp', 'tm', None, 'mp')
- grad_w_query: float32 [4096, 2048], P(('dp', 'tm'), 'mp')
- grad_w_key: float32 [4096, 2048], P(('dp', 'tm'), 'mp')
- grad_w_value: float32 [4096, 2048], P(('dp', 'tm'), 'mp')
- grad_w_out: float32 [2048, 4096], P('mp', ('dp', 'tm'))
The draws below stay inside these ranges and needn't reach their ends.
Inputs may be any that keep to these rules, and one draw needn't show every extreme that they name: Frame f of clip c reads stored span (f) * 2 + frame_span[c, f] of the same clip; each span is read by at most one frame, and a span that no frame reads gets zero gradient.
All inputs are finite; a program needn't handle non-finite values.
Results may differ from the reference program's by a relative error of at most 0.03.
The reference program's roundings to bfloat16 on the way (of `frames`, `normed`, `att_grad`, `soft_b`, `att_out` and `dscore`) count: a program that leaves them out, or rounds other values in their place, can miss the bound.
Values may be sent and summed in bfloat16 or wider, within the bound.
A program may use at most 128 MiB of HBM per device.

```python
import jax
import jax.numpy as jnp
from jax import lax

D = 4096
HS = 128
FR_DEV = 1
CH_DEV = 2
PATCH = 256
HD = 2048
CLIPS = 4
FRAMES = 8
SPANS = 16
N_TM = 8


def draw_norm_gain(key, part):
    key = jax.random.fold_in(key, 7)
    lower = jnp.log(0.5)
    upper = jnp.log(2.0)
    values = jnp.exp(jax.random.uniform(key, (D,), jnp.float32, lower, upper))
    return values.astype(jnp.bfloat16)


def set_ends(values, key, smallest, top_value):
    index_at = [jax.random.randint(jax.random.fold_in(key, axis), (), 0, length) for axis, length in enumerate(values.shape)]
    main_axis = values.shape.index(max(values.shape))
    beside = index_at[:main_axis] + [(index_at[main_axis] + 1) % values.shape[main_axis]] + index_at[main_axis + 1:]
    return values.at[tuple(index_at)].set(smallest).at[tuple(beside)].set(top_value)


def block_scale(key, extent, cuts, smallest, top_value):
    level, own = 1.0, jax.random.fold_in(key, 6)
    for position, blocks in cuts:
        heights = jnp.exp(jax.random.uniform(jax.random.fold_in(own, position), (blocks,), jnp.float32, smallest / len(cuts), top_value / len(cuts)))
        level = level * jnp.repeat(heights, extent[position] // blocks).reshape([-1 if axis == position else 1 for axis in range(len(extent))])
    return level


def bell_draw(rng, shape, scale, reach, shards=(), held_as=jnp.bfloat16):
    loudness = block_scale(rng, shape, shards, -0.22, 0.18) if shards else 1.0
    drawn = jax.random.normal(rng, shape, jnp.float32) * scale * loudness
    return jnp.minimum(jnp.maximum(drawn, -reach), reach).astype(held_as)


def setup_inputs(seed: int = 0) -> dict:
    key_of = jax.random.split(jax.random.key(seed), 9)
    return {
        "spans": bell_draw(key_of[0], (CLIPS, SPANS, PATCH, D), 1.0, 6.0, ((0, 4), (1, 8), (3, 8))),
        "frame_span": set_ends(jax.random.randint(key_of[1], (CLIPS, FRAMES), 0, CH_DEV), jax.random.fold_in(key_of[1], 1), 0, CH_DEV - 1).astype(jnp.int32),
        "norm_gain": draw_norm_gain(jax.random.fold_in(key_of[8], 71), 0),
        "w_query": bell_draw(key_of[3], (D, HD), D ** -0.5, 0.09375, ((0, 32), (1, 8))),
        "w_key": bell_draw(key_of[4], (D, HD), D ** -0.5, 0.09375, ((0, 32), (1, 8))),
        "w_value": bell_draw(key_of[5], (D, HD), D ** -0.5, 0.09375, ((0, 32), (1, 8))),
        "w_out": bell_draw(key_of[6], (HD, D), HD ** -0.5, 0.125, ((0, 8), (1, 32))),
        "grad_out": bell_draw(key_of[7], (CLIPS, FRAMES, PATCH, D), 1.0, 6.0, ((0, 4), (1, 8), (3, 8))),
    }


EPSILON = 1e-05

def product(left, right):
    return jnp.dot(left.astype(jnp.float32), right.astype(jnp.float32), precision=lax.Precision.HIGHEST)

def attend(pieces):
    queries, key_rows, value_rows, att_grad = pieces
    clips, frames_all, patches, width = queries.shape
    heads = width // HS

    def split_heads(array):
        return array.reshape(clips, frames_all, patches, heads, HS).astype(jnp.float32)

    def join_heads(array):
        return array.reshape(clips, frames_all, patches, width)
    query_h = split_heads(queries)
    key_h = split_heads(key_rows)
    value_h = split_heads(value_rows)
    grad_h = split_heads(att_grad)
    scale = HS ** (-0.5)
    scores = jnp.einsum('cfphd,cgphd->cphfg', query_h, key_h, precision=lax.Precision.HIGHEST) * scale
    causal = jnp.arange(frames_all)[:, None] >= jnp.arange(frames_all)[None, :]
    scores = jnp.where(causal, scores, -1e+30)
    peak = lax.optimization_barrier(jnp.max(scores, axis=-1, keepdims=True))
    expo = jnp.exp(scores - peak)
    soft = expo / lax.optimization_barrier(jnp.sum(expo, axis=-1, keepdims=True))
    soft_b = soft.astype(jnp.bfloat16).astype(jnp.float32)
    att_out = jnp.einsum('cphfg,cgphd->cfphd', soft_b, value_h, precision=lax.Precision.HIGHEST).astype(jnp.bfloat16)
    dsoft = jnp.einsum('cfphd,cgphd->cphfg', grad_h, value_h, precision=lax.Precision.HIGHEST)
    dscore = (soft * (dsoft - lax.optimization_barrier(jnp.sum(dsoft * soft, axis=-1, keepdims=True))) * scale).astype(jnp.bfloat16).astype(jnp.float32)
    grad_query = jnp.einsum('cphfg,cgphd->cfphd', dscore, key_h, precision=lax.Precision.HIGHEST).astype(jnp.bfloat16)
    grad_key = jnp.einsum('cphfg,cfphd->cgphd', dscore, query_h, precision=lax.Precision.HIGHEST).astype(jnp.bfloat16)
    grad_value = jnp.einsum('cphfg,cfphd->cgphd', soft_b, grad_h, precision=lax.Precision.HIGHEST).astype(jnp.bfloat16)
    return (join_heads(att_out), join_heads(grad_query), join_heads(grad_key), join_heads(grad_value))

def reference(spans, frame_span, norm_gain, w_query, w_key, w_value, w_out, grad_out):
    slots = (jnp.arange(FRAMES, dtype=jnp.int32) // FR_DEV * CH_DEV)[None, :] + frame_span.astype(jnp.int32)
    frames = jnp.take_along_axis(spans, slots[:, :, None, None], axis=1)
    x_flat = frames.reshape(-1, D).astype(jnp.float32)
    gain = norm_gain.astype(jnp.float32)
    inverse = lax.rsqrt(lax.optimization_barrier(jnp.mean(x_flat * x_flat, axis=1, keepdims=True)) + EPSILON)
    normed = (x_flat * inverse * gain).astype(jnp.bfloat16)
    dy_flat = grad_out.reshape(-1, D)
    queries = product(normed, w_query).astype(jnp.bfloat16)
    key_rows = product(normed, w_key).astype(jnp.bfloat16)
    value_rows = product(normed, w_value).astype(jnp.bfloat16)
    att_grad = product(dy_flat, w_out.T).astype(jnp.bfloat16)
    shape4 = (CLIPS, FRAMES, PATCH, HD)
    outputs = attend((queries.reshape(shape4), key_rows.reshape(shape4), value_rows.reshape(shape4), att_grad.reshape(shape4)))
    att_out = outputs[0].reshape(-1, HD)
    grad_query = outputs[1].reshape(-1, HD)
    grad_key = outputs[2].reshape(-1, HD)
    grad_value = outputs[3].reshape(-1, HD)
    grad_normed = product(grad_query, w_query.T) + product(grad_key, w_key.T) + product(grad_value, w_value.T)
    scaled = grad_normed * gain
    inner = lax.optimization_barrier(jnp.mean(scaled * x_flat, axis=1, keepdims=True))
    branch = inverse * scaled - x_flat * inverse ** 3 * inner
    grad_frames = grad_out.astype(jnp.float32) + branch.reshape(CLIPS, FRAMES, PATCH, D)
    picker = (slots[:, :, None] == jnp.arange(SPANS, dtype=jnp.int32)[None, None, :]).astype(jnp.float32)
    span_grad = jnp.einsum('cfs,cfpd->cspd', picker, grad_frames, precision=lax.Precision.HIGHEST).astype(jnp.bfloat16)
    blocks = CLIPS * N_TM
    rows = FR_DEV * PATCH
    grads_cat = jnp.concatenate([grad_query, grad_key, grad_value], axis=1)

    def accumulate(running, items):
        normed_b, cat_b, dy_b, att_b = items
        proj = product(normed_b.T, cat_b).astype(jnp.bfloat16)
        outer = product(att_b.T, dy_b).astype(jnp.bfloat16)
        proj = lax.optimization_barrier(proj).astype(jnp.float32)
        outer = lax.optimization_barrier(outer).astype(jnp.float32)
        return ((running[0] + proj, running[1] + outer), None)
    init = (jnp.zeros((D, 3 * HD), jnp.float32), jnp.zeros((HD, D), jnp.float32))
    sums, unused = lax.scan(accumulate, init, (normed.reshape(blocks, rows, D), grads_cat.reshape(blocks, rows, 3 * HD), dy_flat.reshape(blocks, rows, D), att_out.reshape(blocks, rows, HD)))
    proj_sum, out_sum = sums
    return (span_grad, proj_sum[:, :HD], proj_sum[:, HD:2 * HD], proj_sum[:, 2 * HD:], out_sum)
```

```python
import jax
import jax.numpy as jnp
from jax import lax
from jax.experimental import pallas as pl
from jax.experimental.pallas import tpu as pltpu
from jax.sharding import PartitionSpec as P

HS = 128
EPSILON = 1e-05
BF = jnp.bfloat16
F32 = jnp.float32
MESH = pl.DeviceIdType.MESH
COPIES = 160

ROWS_COLS = (((1,), (1,)), ((), ()))


def dot(left, right):
    return jnp.dot(left, right, preferred_element_type=F32)


def dot_t(left, right):
    return lax.dot_general(left, right, ROWS_COLS, preferred_element_type=F32)


class Copies:
    def __init__(self, send, recv):
        self.send = send
        self.recv = recv
        self.started = []

    def __call__(self, src, dst, device):
        at = len(self.started)
        assert at < COPIES
        copy = pltpu.make_async_remote_copy(
            src_ref=src,
            dst_ref=dst,
            send_sem=self.send.at[at],
            recv_sem=self.recv.at[at],
            device_id=device,
            device_id_type=MESH,
        )
        copy.start()
        self.started.append(copy)
        return copy


def kernel(
    x_ref,
    dy_ref,
    gain_ref,
    wq_ref,
    wk_ref,
    wv_ref,
    wo_ref,
    gf_ref,
    gq_ref,
    gk_ref,
    gv_ref,
    go_ref,
    xn,
    dy,
    wp,
    wg,
    ss,
    sl,
    iv,
    aq,
    aa,
    sb,
    rb,
    ob,
    gb,
    gc,
    gt,
    ts,
    tr,
    tl,
    tt,
    ps,
    sr,
    po,
    cs,
    cr,
    wt,
    ra,
    ta,
    r1,
    rc,
    tc,
    rf,
    fs,
    fr,
    fh,
    send,
    recv,
):
    dp = lax.axis_index("dp")
    tm = lax.axis_index("tm")
    mp = lax.axis_index("mp")
    core = lax.rem(dp, 2)
    other = 1 - core
    yh = lax.div(dp, 2)
    x = lax.div(tm, 2)
    yl = lax.rem(tm, 2)
    y = yh * 2 + yl

    def device(x_at, y_at):
        return (lax.div(y_at, 2) * 2 + core, x_at * 2 + lax.rem(y_at, 2), mp)

    def ring8(offset):
        return lax.rem(mp + offset + 8, 8)

    def along_z(offset):
        return (dp, tm, ring8(offset))

    def along_tm(offset):
        return (dp, lax.rem(tm + offset, 8), mp)

    sibling = (yh * 2 + other, tm, mp)
    zr, zl = along_z(1), along_z(-1)
    x1, x2, x3 = (lax.rem(x + k, 4) for k in (1, 2, 3))
    y1, y2, y3 = (lax.rem(y + k, 4) for k in (1, 2, 3))
    xr, xl = device(x1, y), device(x3, y)
    yr, yd = device(x, y1), device(x, y3)
    far_y = device(x, lax.rem(y + 3 + 2 * yl, 4))

    def hi(v):
        return lax.div(v, 2)

    def lo(v):
        return lax.rem(v, 2)

    barrier = pltpu.get_barrier_semaphore()
    partners = [sibling, far_y]
    partners += [along_z(k) for k in range(1, 8)]
    partners += [along_tm(k) for k in range(1, 8)]
    for partner in partners:
        pl.semaphore_signal(barrier, inc=1, device_id=partner, device_id_type=MESH)
    pl.semaphore_wait(barrier, len(partners))

    copy = Copies(send, recv)

    class Ring:
        def __init__(self, src, ref):
            self.ref = ref
            home = ref.at[mp, core]
            self.right = copy(src, home, zr)
            self.left = copy(src, home, zl)
            self.pending = [copy(src, home, sibling)]
            self.step = 1

        def advance(self):
            k = self.step
            self.step += 1
            ref = self.ref
            self.right.wait_recv()
            if k < 4:
                block = ref.at[ring8(-k), core]
                part = block if k < 3 else block.at[pl.ds(0, 128)]
                self.right = copy(part, part, zr)
                self.pending.append(copy(block, block, sibling))
            self.left.wait_recv()
            if k < 4:
                block = ref.at[ring8(k), core]
                part = block if k < 3 else block.at[pl.ds(128, 128)]
                self.left = copy(part, part, zl)
                self.pending.append(copy(block, block, sibling))
            else:
                block = ref.at[ring8(4), core]
                self.pending.append(copy(block, block, sibling))

        def settle(self):
            for c in self.pending:
                c.wait_recv()
            self.pending = []

    ring_dy = Ring(dy_ref, dy)

    for h in range(2):
        for a, ref in enumerate((wq_ref, wk_ref, wv_ref)):
            wp[h, :, a * HS : (a + 1) * HS] = ref[:, h * HS : (h + 1) * HS]
        wp[h, :, 3 * HS :] = wo_ref[h * HS : (h + 1) * HS, :].astype(F32).T.astype(BF)
    xh, xlo = hi(x), lo(x)
    mine = wg.at[yh, core, xh, xlo, yl]
    pair = copy(wp.at[other], mine, sibling)

    sums = jnp.zeros((256, HS), F32)
    for g in range(4):
        part = x_ref[:, g * HS : (g + 1) * HS].astype(F32)
        sums = sums + part * part
    row = jnp.sum(sums.T, axis=0, keepdims=True)
    sl[...] = jnp.broadcast_to(row, (8, 256))
    sumsq = [copy(sl, ss.at[mp], along_z(k)) for k in range(1, 8)]
    ss[mp] = sl[...]
    wg[yh, core, xh, xlo, yl] = wp[core]
    dy[mp, core] = dy_ref[...]

    pair.wait_recv()

    def block(x_at, y_at, s):
        return wg.at[hi(y_at), s, hi(x_at), lo(x_at), lo(y_at)]

    def upper(ref):
        return ref.at[pl.ds(0, 64)]

    def lower(ref):
        return ref.at[pl.ds(64, 64)]

    own_a, own_b = block(x, y, 0), block(x, y, 1)
    a_r, a_l = copy(own_a, own_a, xr), copy(own_a, own_a, xl)
    b_r, b_l = copy(own_b, own_b, yr), copy(own_b, own_b, yd)

    for c in sumsq:
        c.wait_recv()
    total = ss[0]
    for k in range(1, 8):
        total = total + ss[k]
    inv_row = lax.rsqrt(total / 4096.0 + EPSILON)
    iv[...] = jnp.broadcast_to(inv_row[0:1, :], (HS, 256)).T
    for g in range(4):
        cols = slice(g * HS, (g + 1) * HS)
        xn[mp, core, :, cols] = (
            x_ref[:, cols].astype(F32) * iv[...] * gain_ref[:, cols].astype(F32)
        ).astype(BF)
    ring_xn = Ring(xn.at[mp, core], xn)

    a_r.wait_recv()
    near = upper(block(x3, y, 0))
    a_r = copy(near, near, xr)
    a_l.wait_recv()
    near = lower(block(x1, y, 0))
    a_l = copy(near, near, xl)
    b_r.wait_recv()
    near = upper(block(x, y3, 1))
    b_r = copy(near, near, yr)
    b_l.wait_recv()
    near = lower(block(x, y1, 1))
    b_l = copy(near, near, yd)

    aq[...] = jnp.zeros_like(aq)
    aa[...] = jnp.zeros_like(aa)

    ring_dy.advance()

    for c in (a_r, a_l, b_r, b_l):
        c.wait_recv()

    def row_a(y_at):
        return wg.at[hi(y_at), 0, :, :, lo(y_at)]

    def row_b(x_at):
        return wg.at[:, 1, hi(x_at), lo(x_at), :]

    a_r, a_l = copy(row_a(y), row_a(y), yr), copy(row_a(y), row_a(y), yd)
    b_r, b_l = copy(row_b(x), row_b(x), xr), copy(row_b(x), row_b(x), xl)

    ring_xn.advance()
    ring_dy.advance()

    a_r.wait_recv()
    near = row_a(y3).at[0]
    a_r = copy(near, near, yr)
    a_l.wait_recv()
    near = row_a(y1).at[1]
    a_l = copy(near, near, yd)
    b_r.wait_recv()
    near = row_b(x3).at[0]
    b_r = copy(near, near, xr)
    b_l.wait_recv()
    near = row_b(x1).at[1]
    b_l = copy(near, near, xl)

    ring_xn.advance()
    ring_dy.advance()

    for c in (a_r, a_l, b_r, b_l):
        c.wait_recv()

    def weights(m, cols):
        return wg[lax.div(m, 4), lo(hi(m)), lo(m), :, :, :, cols].reshape(512, -1)

    qkv_cols = slice(0, 3 * HS)
    out_cols = slice(3 * HS, 4 * HS)

    def forward(ref, into, cols, first, step, count):
        def body(i, carry):
            m = ring8(first + step * i)
            w = weights(m, cols)
            for s in range(2):
                into[s] += dot(ref[m, s], w)
            return carry

        lax.fori_loop(0, count, body, 0)

    def forward_dy(*which):
        ring_dy.settle()
        forward(dy, aa, out_cols, *which)

    def forward_xn(*which):
        ring_xn.settle()
        forward(xn, aq, qkv_cols, *which)

    forward_dy(-2, 1, 5)
    forward_xn(-1, 1, 3)
    ring_xn.advance()
    forward_xn(-2, 4, 2)
    ring_dy.advance()
    forward_dy(-3, 6, 2)
    ring_xn.advance()
    forward_xn(-3, 6, 2)
    forward_dy(4, 0, 1)
    forward_xn(4, 0, 1)

    for s in range(2):
        for a in range(3):
            sb[a, s] = aq[s, :, a * HS : (a + 1) * HS].astype(BF)
        sb[3, s] = aa[s].astype(BF)

    def patch_rows(at):
        return pl.ds(pl.multiple_of(at * 32, 32), 32)

    trips = []
    for k in range(1, 8):
        to = lax.rem(tm + k, 8)
        trips.append(copy(sb.at[:, :, patch_rows(to)], rb.at[:, :, tm], along_tm(k)))
    rb[:, :, tm] = sb[:, :, patch_rows(tm), :]
    for c in trips:
        c.wait_recv()

    row_id = lax.broadcasted_iota(jnp.int32, (256, 256), 0)
    col_id = lax.broadcasted_iota(jnp.int32, (256, 256), 1)
    seen = ((row_id & 31) == (col_id & 31)) & ((row_id >> 5) >= (col_id >> 5))
    scale = HS ** (-0.5)
    for s in range(2):
        q, k, v, a = (rb[i, s].reshape(256, HS) for i in range(4))
        scores = jnp.where(seen, dot_t(q, k) * scale, -1e30)
        expo = jnp.exp(scores - jnp.max(scores, axis=1, keepdims=True))
        soft = expo / jnp.sum(expo, axis=1, keepdims=True)
        soft_b = soft.astype(BF)
        dsoft = dot_t(a, v)
        dscore = soft * (dsoft - jnp.sum(dsoft * soft, axis=1, keepdims=True)) * scale
        dscore_b = dscore.astype(BF)
        results = (
            dot(soft_b, v),
            dot(dscore_b, k),
            dot(dscore.T.astype(BF), q),
            dot(soft.T.astype(BF), a),
        )
        for i, value in enumerate(results):
            ob[i, s] = value.astype(BF).reshape(8, 32, HS)

    trips = []
    for k in range(1, 8):
        to = lax.rem(tm + k, 8)
        trips.append(copy(ob.at[:, :, to], gb.at[:, :, patch_rows(tm)], along_tm(k)))
    gb[:, :, patch_rows(tm), :] = ob[:, :, tm]
    for c in trips:
        c.wait_recv()

    for s in range(2):
        for a in range(3):
            gc[s, :, a * HS : (a + 1) * HS] = gb[1 + a, s]

    def input_grad(index, offset):
        m = ring8(offset)
        w = weights(m, qkv_cols)
        ps[index] = dot_t(gc[other], w).astype(BF)
        po[index] = dot_t(gc[core], w)
        return copy(ps.at[index], sr.at[index], sibling)

    def total_of(index, rows):
        return po[index, rows, :] + sr[index, rows, :].astype(F32)

    offsets = (4, 3, -3, 2, -2, 1, -1, 0)
    across = [input_grad(i, offsets[i]) for i in range(3)]

    for s in range(2):
        for a in range(4):
            source = gb[(a + 1) % 4, s]
            gt[a * HS : (a + 1) * HS, s * 256 : (s + 1) * 256] = source.astype(F32).T.astype(BF)

    def weight_grad(yh_at, s_at, xh_at):
        m = (yh_at * 2 + s_at) * 2 + xh_at
        first = dot(gt[: 3 * HS, :], xn[m].reshape(512, 512)).astype(BF)
        second = dot(gt[3 * HS :, :], dy[m].reshape(512, 512)).astype(BF)
        for i in range(4):
            cols = slice(i * HS, (i + 1) * HS)
            wt[yh_at, s_at, xh_at, i // 2, i % 2, : 3 * HS, :] = first[:, cols]
            wt[yh_at, s_at, xh_at, i // 2, i % 2, 3 * HS :, :] = second[:, cols]

    def far_grads(i, carry):
        weight_grad(1 - yh, 0, i)
        weight_grad(i, 1, 1 - xh)
        return carry

    lax.fori_loop(0, 2, far_grads, 0)

    class Scatter:
        def __init__(self, part, right, left, got, tmp, at):
            self.part = part
            self.right = right
            self.left = left
            self.got = got
            self.tmp = tmp
            self.at = at

        def begin(self):
            _, _, two, _ = self.at
            self.r2 = copy(self.part(two, 0), self.got.at[0], self.right)
            self.l2 = copy(self.part(two, 1), self.got.at[1], self.left)

        def near(self):
            _, one, _, three = self.at
            self.r1 = copy(self.part(one, 1), self.got.at[2], self.right)
            self.l1 = copy(self.part(three, 0), self.got.at[3], self.left)

        def chain(self):
            _, one, _, three = self.at
            self.r2.wait_recv()
            self.tmp[0] = (self.part(one, 0)[...].astype(F32) + self.got[0].astype(F32)).astype(BF)
            self.r3 = copy(self.tmp.at[0], self.got.at[4], self.right)
            self.l2.wait_recv()
            self.tmp[1] = (self.part(three, 1)[...].astype(F32) + self.got[1].astype(F32)).astype(BF)
            self.l3 = copy(self.tmp.at[1], self.got.at[5], self.left)

        def finish(self):
            here = self.at[0]
            got = self.got
            self.l1.wait_recv()
            self.r3.wait_recv()
            first = self.part(here, 0)[...].astype(F32) + got[3].astype(F32) + got[4].astype(F32)
            self.r1.wait_recv()
            self.l3.wait_recv()
            second = self.part(here, 1)[...].astype(F32) + got[2].astype(F32) + got[5].astype(F32)
            return first, second

    xs, ys = (x, x1, x2, x3), (y, y1, y2, y3)
    sc_a = Scatter(
        lambda v, half: wt.at[hi(v), 0, half, :, lo(v)], yr, yd, ra.at[0], ta.at[0], ys
    )
    sc_b = Scatter(
        lambda v, half: wt.at[half, 1, hi(v), lo(v), :], xr, xl, ra.at[1], ta.at[1], xs
    )
    sc_a.begin()
    sc_b.begin()

    way_r = ((4, 0), (3, 1), (3, 0), (2, 1), (2, 0), (1, 1), (1, 0))
    way_l = ((4, 1), (3, 0), (3, 1), (2, 0), (2, 1), (1, 0), (1, 1))
    flying = {}

    def hop(direction, order):
        way, sign, to = ((way_r, 1, zr), (way_l, -1, zl))[direction]
        distance, half = way[order]
        offset = sign * distance if distance < 4 else 4
        index = offsets.index(offset)
        rows = slice(half * 128, half * 128 + 128)
        value = total_of(index, rows)
        before = (distance + 1, half)
        if before in way:
            prior = way.index(before)
            flying[direction, prior].wait_recv()
            value = value + cr[direction, prior].astype(F32)
        cs[direction, order] = value.astype(BF)
        flying[direction, order] = copy(cs.at[direction, order], cr.at[direction, order], to)

    across += [input_grad(i, offsets[i]) for i in range(3, 8)]
    for i in range(3):
        across[i].wait_recv()
    for order in range(2):
        hop(0, order)
        hop(1, order)

    def near_grads(i, carry):
        weight_grad(yh, 0, i)
        weight_grad(i, 1, xh)
        return carry

    lax.fori_loop(0, 2, near_grads, 0)
    sc_a.near()
    sc_b.near()

    for s in range(2):
        prod = jnp.zeros((256, HS), F32)
        for a in range(3):
            prod = prod + gb[1 + a, s].astype(F32) * sb[a, s].astype(F32)
        ts[s] = jnp.broadcast_to(jnp.sum(prod.T, axis=0, keepdims=True), (8, 256))
    inner_pair = copy(ts.at[other], tr, sibling)

    for i in range(3, 8):
        across[i].wait_recv()
    hop(0, 2)
    hop(1, 2)
    inner_pair.wait_recv()
    tl[...] = ts[core] + tr[...]
    tt[mp] = tl[...]
    inner = [copy(tl, tt.at[mp], along_z(k)) for k in range(1, 8)]
    sc_a.chain()
    sc_b.chain()
    for order in (3, 4):
        hop(0, order)
        hop(1, order)

    sc2 = []
    for index, (sc, right, left, at) in enumerate(((sc_a, xr, xl, xs), (sc_b, yr, yd, ys))):
        first, second = sc.finish()
        r1[index, 0] = first.astype(BF)
        r1[index, 1] = second.astype(BF)

        def part(v, half, index=index):
            return r1.at[index, hi(v), lo(v), pl.ds(half * 256, 256)]

        stage = Scatter(part, right, left, rc.at[index], tc.at[index], at)
        stage.begin()
        stage.near()
        sc2.append(stage)

    for order in (5, 6):
        hop(0, order)
        hop(1, order)
    for stage in sc2:
        stage.chain()
    for index, stage in enumerate(sc2):
        first, second = stage.finish()
        rf[index, 0:256, :] = first
        rf[index, 256:512, :] = second
    fs[...] = rf[other].astype(BF)
    last = copy(fs, fr, sibling)
    fh[core] = rf[core]

    for c in inner:
        c.wait_recv()
    inner_row = tt[0]
    for k in range(1, 8):
        inner_row = inner_row + tt[k]
    inner_col = jnp.broadcast_to(inner_row[0:1, :] / 4096.0, (HS, 256)).T
    for direction, order in ((0, 5), (0, 6), (1, 5), (1, 6)):
        flying[direction, order].wait_recv()
    for half in range(2):
        rows = slice(half * 128, half * 128 + 128)
        grad = total_of(7, rows)
        for direction, way in enumerate((way_r, way_l)):
            grad = grad + cr[direction, way.index((1, half))].astype(F32)
        inverse = iv[rows, :]
        back = inverse * inverse * inner_col[rows, :]
        for g in range(4):
            cols = slice(g * HS, (g + 1) * HS)
            scaled = grad[:, cols] * gain_ref[:, cols].astype(F32)
            branch = inverse * scaled - x_ref[rows, cols].astype(F32) * back
            gf_ref[rows, cols] = (dy_ref[rows, cols].astype(F32) + branch).astype(BF)

    last.wait_recv()
    fh[other] = fr[...].astype(F32)
    for h in range(2):
        cols = slice(h * HS, (h + 1) * HS)
        for a, ref in enumerate((gq_ref, gk_ref, gv_ref)):
            ref[:, cols] = fh[h, a * HS : (a + 1) * HS, :].T
        go_ref[cols, :] = fh[h, 3 * HS :, :]

    for c in copy.started:
        c.wait_send()


def local(spans, frame_span, norm_gain, w_query, w_key, w_value, w_out, grad_out):
    chosen = frame_span[0, 0] == 0
    frames = jnp.where(chosen, spans[0, 0], spans[0, 1])
    vmem = pl.BlockSpec(memory_space=pltpu.VMEM)
    shape = jax.ShapeDtypeStruct
    scratch = [
        ((8, 2, 256, 512), BF),
        ((8, 2, 256, 512), BF),
        ((2, 128, 512), BF),
        ((2, 2, 2, 2, 2, 128, 512), BF),
        ((8, 8, 256), F32),
        ((8, 256), F32),
        ((256, 128), F32),
        ((2, 256, 384), F32),
        ((2, 256, 128), F32),
        ((4, 2, 256, 128), BF),
        ((4, 2, 8, 32, 128), BF),
        ((4, 2, 8, 32, 128), BF),
        ((4, 2, 256, 128), BF),
        ((2, 256, 384), BF),
        ((512, 512), BF),
        ((2, 8, 256), F32),
        ((8, 256), F32),
        ((8, 256), F32),
        ((8, 8, 256), F32),
        ((8, 256, 512), BF),
        ((8, 256, 512), BF),
        ((8, 256, 512), F32),
        ((2, 7, 128, 512), BF),
        ((2, 7, 128, 512), BF),
        ((2, 2, 2, 2, 2, 512, 128), BF),
        ((2, 6, 2, 512, 128), BF),
        ((2, 2, 2, 512, 128), BF),
        ((2, 2, 2, 512, 128), BF),
        ((2, 6, 256, 128), BF),
        ((2, 2, 256, 128), BF),
        ((2, 512, 128), F32),
        ((512, 128), BF),
        ((512, 128), BF),
        ((2, 512, 128), F32),
    ]
    grad_frames, grad_q, grad_k, grad_v, grad_o = pl.pallas_call(
        kernel,
        out_shape=(
            shape((256, 512), BF),
            shape((128, 256), F32),
            shape((128, 256), F32),
            shape((128, 256), F32),
            shape((256, 128), F32),
        ),
        in_specs=[vmem] * 7,
        out_specs=(vmem,) * 5,
        scratch_shapes=[pltpu.VMEM(*each) for each in scratch]
        + [pltpu.SemaphoreType.DMA((COPIES,)), pltpu.SemaphoreType.DMA((COPIES,))],
        compiler_params=pltpu.CompilerParams(
            collective_id=0, has_side_effects=True, vmem_limit_bytes=56 * 1024 * 1024
        ),
    )(frames, grad_out[0, 0], norm_gain[None, :], w_query, w_key, w_value, w_out)
    which = jnp.arange(2, dtype=jnp.int32)[:, None, None]
    span_grad = jnp.where(which == frame_span[0, 0], grad_frames[None], jnp.zeros((), BF))
    return span_grad[None], grad_q, grad_k, grad_v, grad_o


def solution(mesh):
    placed = (
        P("dp", "tm", None, "mp"),
        P("dp", "tm"),
        P("mp"),
        P(("dp", "tm"), "mp"),
        P(("dp", "tm"), "mp"),
        P(("dp", "tm"), "mp"),
        P("mp", ("dp", "tm")),
        P("dp", "tm", None, "mp"),
    )
    return jax.shard_map(
        local,
        mesh=mesh,
        in_specs=placed,
        out_specs=(
            P("dp", "tm", None, "mp"),
            P(("dp", "tm"), "mp"),
            P(("dp", "tm"), "mp"),
            P(("dp", "tm"), "mp"),
            P("mp", ("dp", "tm")),
        ),
        check_vma=False,
    )
```

```python
import jax
import jax.numpy as jnp
from jax import lax
from jax.experimental import pallas as pl
from jax.experimental.pallas import tpu as pltpu
from jax.sharding import PartitionSpec as P

HS = 128
EPSILON = 1e-05
BF = jnp.bfloat16
F32 = jnp.float32
MESH = pl.DeviceIdType.MESH
COPIES = 230

ROWS_COLS = (((1,), (1,)), ((), ()))


def dot(left, right):
    return jnp.dot(left, right, preferred_element_type=F32)


def dot_t(left, right):
    return lax.dot_general(left, right, ROWS_COLS, preferred_element_type=F32)


class Copies:
    def __init__(self, send, recv):
        self.send = send
        self.recv = recv
        self.started = []

    def __call__(self, src, dst, device):
        at = len(self.started)
        assert at < COPIES
        copy = pltpu.make_async_remote_copy(
            src_ref=src,
            dst_ref=dst,
            send_sem=self.send.at[at],
            recv_sem=self.recv.at[at],
            device_id=device,
            device_id_type=MESH,
        )
        copy.start()
        self.started.append(copy)
        return copy


def kernel(
    spans_ref,
    which_ref,
    gain_ref,
    wq_ref,
    wk_ref,
    wv_ref,
    wo_ref,
    dy_ref,
    span_out,
    q_out,
    k_out,
    v_out,
    o_out,
    sp,
    xs_in,
    xn,
    dy,
    wl,
    wol,
    wp,
    wg,
    ss,
    sl,
    iv,
    aq,
    aa,
    sb,
    rb,
    so,
    st,
    ob,
    gb,
    gc,
    gt,
    ts,
    tr,
    tl,
    tt,
    ps,
    sr,
    po,
    cs,
    cr,
    wt,
    ra,
    ta,
    r1,
    rc,
    tc,
    rf,
    fs,
    fr,
    fh,
    span_v,
    g_v,
    o_v,
    send,
    recv,
    near_sem,
):
    dp = lax.axis_index("dp")
    tm = lax.axis_index("tm")
    mp = lax.axis_index("mp")
    core = lax.rem(dp, 2)
    other = 1 - core
    yh = lax.div(dp, 2)
    x = lax.div(tm, 2)
    yl = lax.rem(tm, 2)
    y = yh * 2 + yl

    def hi(v):
        return lax.div(v, 2)

    def lo(v):
        return lax.rem(v, 2)

    def device(x_at, y_at):
        return (hi(y_at) * 2 + core, x_at * 2 + lo(y_at), mp)

    def ring8(offset):
        return lax.rem(mp + offset + 8, 8)

    def along_z(offset):
        return (dp, tm, ring8(offset))

    def along_tm(offset):
        return (dp, lax.rem(tm + offset, 8), mp)

    sibling = (yh * 2 + other, tm, mp)
    zr, zl = along_z(1), along_z(-1)
    xs = tuple(lax.rem(x + k, 4) for k in range(4))
    ys = tuple(lax.rem(y + k, 4) for k in range(4))
    xh = hi(x)
    xr, xl = device(xs[1], y), device(xs[3], y)
    yr, yd = device(x, ys[1]), device(x, ys[3])
    far_y = device(x, lax.rem(y + 3 + 2 * yl, 4))

    fetched = []

    def fetch(src, dst):
        c = pltpu.make_async_copy(src, dst, near_sem.at[len(fetched)])
        c.start()
        fetched.append(c)
        return c

    span_in = fetch(spans_ref.at[0], sp)
    w_in = [fetch(ref, wl.at[a]) for a, ref in enumerate((wq_ref, wk_ref, wv_ref))]
    w_in.append(fetch(wo_ref, wol))
    dy_in = fetch(dy_ref.at[0, 0], dy.at[mp, core])

    barrier = pltpu.get_barrier_semaphore()
    partners = [sibling, far_y]
    partners += [along_z(k) for k in range(1, 8)]
    partners += [along_tm(k) for k in range(1, 8)]
    for partner in partners:
        pl.semaphore_signal(barrier, inc=1, device_id=partner, device_id_type=MESH)

    which = which_ref[0, 0]
    gain = gain_ref[...].astype(F32)
    span_in.wait()
    xs_in[...] = jnp.where(which == 0, sp[0], sp[1])
    sums = jnp.zeros((256, HS), F32)
    for g in range(4):
        part = xs_in[:, g * HS : (g + 1) * HS].astype(F32)
        sums = sums + part * part
    row = jnp.sum(sums.T, axis=0, keepdims=True)
    sl[...] = jnp.broadcast_to(row, (8, 256))
    for c in w_in:
        c.wait()
    for h in range(2):
        for a in range(3):
            wp[h, :, a * HS : (a + 1) * HS] = wl[a, :, h * HS : (h + 1) * HS]
        wp[h, :, 3 * HS :] = wol[h * HS : (h + 1) * HS, :].astype(F32).T.astype(BF)
    dy_in.wait()

    pl.semaphore_wait(barrier, len(partners))

    copy = Copies(send, recv)

    gather_ways = (
        (((1, 0), (1, 1), (2, 0), (2, 1), (3, 0), (3, 1), (4, 0)), -1, zr),
        (((1, 1), (1, 0), (2, 1), (2, 0), (3, 1), (3, 0), (4, 1)), 1, zl),
    )

    class Ring:
        def __init__(self, ref):
            self.ref = ref
            self.flight = {}
            home = ref.at[mp, core]
            self.home = home
            self.pending = []

        def begin(self):
            for j in range(2):
                self.pass_on(0, j)
                self.pass_on(1, j)
            self.pending.append(copy(self.home, self.home, sibling))

        def pass_on(self, d, j):
            way, sign, to = gather_ways[d]
            k, half = way[j]
            part = self.ref.at[ring8(sign * (k - 1)), core, pl.ds(half * 128, 128)]
            self.flight[d, j] = copy(part, part, to)

        def take(self, j, forward=True):
            for d in range(2):
                way, sign, _ = gather_ways[d]
                k, half = way[j]
                self.flight[d, j].wait_recv()
                if forward and j + 2 < 7:
                    self.pass_on(d, j + 2)
                part = self.ref.at[ring8(sign * k), core, pl.ds(half * 128, 128)]
                self.pending.append(copy(part, part, sibling))

        def settle(self):
            for c in self.pending:
                c.wait_recv()
            self.pending = []

    class Spread:
        def __init__(self, at, ring, right, left):
            self.at = at
            self.ring = ring
            self.to = (right, left)
            own = at(ring[0])
            self.r = copy(own, own, right)
            self.l = copy(own, own, left)

        def relay(self):
            self.r.wait_recv()
            part = self.at(self.ring[3]).at[pl.ds(0, 64)]
            self.r = copy(part, part, self.to[0])
            self.l.wait_recv()
            part = self.at(self.ring[1]).at[pl.ds(64, 64)]
            self.l = copy(part, part, self.to[1])

        def done(self):
            self.r.wait_recv()
            self.l.wait_recv()

    ring_dy = Ring(dy)
    ring_xn = Ring(xn)

    sumsq = [copy(sl, ss.at[mp], along_z(k)) for k in range(1, 8)]
    mine = wg.at[yh, core, xh, lo(x), yl]
    pair = copy(wp.at[other], mine, sibling)
    ring_dy.begin()
    ss[mp] = sl[...]
    wg[yh, core, xh, lo(x), yl] = wp[core]
    aq[...] = jnp.zeros_like(aq)
    aa[...] = jnp.zeros_like(aa)

    def block(x_at, y_at, s):
        return wg.at[hi(y_at), s, hi(x_at), lo(x_at), lo(y_at)]

    def spread_a(k):
        return Spread(lambda v: block(xs[k], v, 0), ys, yr, yd)

    def spread_b(k):
        return Spread(lambda v: block(v, ys[k], 1), xs, xr, xl)

    pair.wait_recv()
    a1 = Spread(lambda v: block(v, y, 0), xs, xr, xl)
    b1 = Spread(lambda v: block(x, v, 1), ys, yr, yd)
    second = {0: (spread_a(0), spread_b(0))}

    for c in sumsq:
        c.wait_recv()
    total = ss[0]
    for k in range(1, 8):
        total = total + ss[k]
    inv_row = lax.rsqrt(total / 4096.0 + EPSILON)
    iv[...] = jnp.broadcast_to(inv_row[0:1, :], (HS, 256)).T
    for g in range(4):
        cols = slice(g * HS, (g + 1) * HS)
        xn[mp, core, :, cols] = (
            xs_in[:, cols].astype(F32) * iv[...] * gain[:, cols]
        ).astype(BF)
    ring_xn.begin()

    a1.relay()
    b1.relay()
    for k in (3, 1):
        second[k] = (spread_a(k), spread_b(k))

    def relay(k):
        second[k][0].relay()
        second[k][1].relay()

    relay(0)
    ring_xn.take(0)
    a1.done()
    b1.done()
    second[2] = (spread_a(2), spread_b(2))
    ring_dy.take(0, forward=False)
    ring_dy.take(1, forward=False)
    ring_xn.take(1)
    relay(3)
    ring_xn.take(2)
    relay(1)
    ring_xn.take(3)
    relay(2)
    ring_xn.take(4)
    for j in (2, 3):
        ring_dy.pass_on(0, j)
        ring_dy.pass_on(1, j)
    ring_xn.take(5)
    for k in range(4):
        second[k][0].done()
        second[k][1].done()

    def weights(m, cols):
        return wg[lax.div(m, 4), lo(hi(m)), lo(m), :, :, :, cols].reshape(512, -1)

    qkv_cols = slice(0, 3 * HS)
    out_cols = slice(3 * HS, 4 * HS)

    def forward(ref, into, cols, first, step, count):
        def body(i, carry):
            m = ring8(first + step * i)
            w = weights(m, cols)
            for s in range(2):
                into[s] += dot(ref[m, s], w)
            return carry

        lax.fori_loop(0, count, body, 0)

    def forward_dy(*which_chunks):
        ring_dy.settle()
        forward(dy, aa, out_cols, *which_chunks)

    def forward_xn(*which_chunks):
        ring_xn.settle()
        forward(xn, aq, qkv_cols, *which_chunks)

    forward_xn(-2, 1, 5)
    ring_xn.take(6)
    forward_xn(-3, 6, 2)
    forward_xn(4, 0, 1)

    def patch_rows(at):
        return pl.ds(pl.multiple_of(at * 32, 32), 32)

    def swap_out(first, count):
        arrays = pl.ds(first, count)
        trips = []
        for k in range(1, 8):
            to = lax.rem(tm + k, 8)
            trips.append(
                copy(sb.at[arrays, :, patch_rows(to)], rb.at[arrays, :, tm], along_tm(k))
            )
        rb[arrays, :, tm] = sb[arrays, :, patch_rows(tm), :]
        return trips

    def swap_back(first, count):
        arrays = pl.ds(first, count)
        trips = []
        for k in range(1, 8):
            to = lax.rem(tm + k, 8)
            trips.append(
                copy(ob.at[arrays, :, to], gb.at[arrays, :, patch_rows(tm)], along_tm(k))
            )
        gb[arrays, :, patch_rows(tm), :] = ob[arrays, :, tm]
        return trips

    def arrive(trips):
        for c in trips:
            c.wait_recv()

    for s in range(2):
        for a in range(3):
            sb[a, s] = aq[s, :, a * HS : (a + 1) * HS].astype(BF)
    trips = swap_out(0, 3)

    ring_dy.take(2)
    forward_dy(-1, 1, 3)
    ring_dy.take(3)
    arrive(trips)

    row_id = lax.broadcasted_iota(jnp.int32, (256, 256), 0)
    col_id = lax.broadcasted_iota(jnp.int32, (256, 256), 1)
    seen = ((row_id & 31) == (col_id & 31)) & ((row_id >> 5) >= (col_id >> 5))
    scale = HS ** (-0.5)
    for s in range(2):
        q, k, v = (rb[i, s].reshape(256, HS) for i in range(3))
        scores = jnp.where(seen, dot_t(q, k) * scale, -1e30)
        expo = jnp.exp(scores - jnp.max(scores, axis=1, keepdims=True))
        soft = expo / jnp.sum(expo, axis=1, keepdims=True)
        so[s] = soft
        st[s] = soft.T.astype(BF)
        ob[0, s] = dot(soft.astype(BF), v).astype(BF).reshape(8, 32, HS)
    att_trips = swap_back(0, 1)

    forward_dy(-2, 4, 2)
    ring_dy.take(4)
    ring_dy.take(5)
    forward_dy(-3, 6, 2)
    ring_dy.take(6)
    forward_dy(4, 0, 1)

    for s in range(2):
        sb[3, s] = aa[s].astype(BF)
    trips = swap_out(3, 1)

    def keep_transposed(a):
        for s in range(2):
            source = gb[(a + 1) % 4, s]
            gt[a * HS : (a + 1) * HS, s * 256 : (s + 1) * 256] = source.astype(F32).T.astype(BF)

    def spread_columns(value, yh_at, s_at, xh_at, rows):
        for i in range(4):
            wt[yh_at, s_at, xh_at, i // 2, i % 2, rows, :] = value[:, i * HS : (i + 1) * HS]

    def out_grad(m, carry):
        value = dot(gt[3 * HS :, :], dy[m].reshape(512, 512)).astype(BF)
        spread_columns(value, lax.div(m, 4), lo(hi(m)), lo(m), out_cols)
        return carry

    arrive(att_trips)
    keep_transposed(3)
    arrive(trips)
    for s in range(2):
        q, k, v, a = (rb[i, s].reshape(256, HS) for i in range(4))
        soft = so[s]
        dsoft = dot_t(a, v)
        dscore = soft * (dsoft - jnp.sum(dsoft * soft, axis=1, keepdims=True)) * scale
        results = (
            dot(dscore.astype(BF), k),
            dot(dscore.T.astype(BF), q),
            dot(st[s], a),
        )
        for i, value in enumerate(results):
            ob[1 + i, s] = value.astype(BF).reshape(8, 32, HS)
    trips = swap_back(1, 3)
    lax.fori_loop(0, 8, out_grad, 0)
    arrive(trips)

    for s in range(2):
        for a in range(3):
            gc[s, :, a * HS : (a + 1) * HS] = gb[1 + a, s]

    def input_grad(index):
        w = weights(ring8(offsets[index]), qkv_cols)
        ps[index] = dot_t(gc[other], w).astype(BF)
        po[index] = dot_t(gc[core], w)
        return copy(ps.at[index], sr.at[index], sibling)

    def total_of(index, rows):
        return po[index, rows, :] + sr[index, rows, :].astype(F32)

    offsets = (4, 3, -3, 2, -2, 1, -1, 0)
    across = [input_grad(0)]

    for a in range(3):
        keep_transposed(a)

    def weight_grad(yh_at, s_at, xh_at):
        m = (yh_at * 2 + s_at) * 2 + xh_at
        value = dot(gt[: 3 * HS, :], xn[m].reshape(512, 512)).astype(BF)
        spread_columns(value, yh_at, s_at, xh_at, qkv_cols)

    def grads(which_chunk):
        def body(i, carry):
            weight_grad(*which_chunk(i))
            return carry

        lax.fori_loop(0, 2, body, 0)

    def half_rows(half):
        return slice(half * 256, half * 256 + 256)

    class Reduce:
        def __init__(self, part, right, left, got, tmp):
            self.part = part
            self.to = (right, left)
            self.got = got
            self.tmp = tmp

        def far(self):
            self.r2 = copy(self.part(2, 0), self.got.at[0], self.to[0])
            self.l2 = copy(self.part(2, 1), self.got.at[1], self.to[1])

        def near(self):
            self.r1 = copy(self.part(1, 1), self.got.at[2], self.to[0])
            self.l1 = copy(self.part(3, 0), self.got.at[3], self.to[1])

        def chain(self):
            self.r2.wait_recv()
            self.tmp[0] = (self.part(1, 0)[...].astype(F32) + self.got[0].astype(F32)).astype(BF)
            self.r3 = copy(self.tmp.at[0], self.got.at[4], self.to[0])
            self.l2.wait_recv()
            self.tmp[1] = (self.part(3, 1)[...].astype(F32) + self.got[1].astype(F32)).astype(BF)
            self.l3 = copy(self.tmp.at[1], self.got.at[5], self.to[1])

        def finish(self):
            got = self.got
            self.l1.wait_recv()
            self.r3.wait_recv()
            first = self.part(0, 0)[...].astype(F32) + got[3].astype(F32) + got[4].astype(F32)
            self.r1.wait_recv()
            self.l3.wait_recv()
            second = self.part(0, 1)[...].astype(F32) + got[2].astype(F32) + got[5].astype(F32)
            return first, second

    def first_stage(axis, k):
        def part_a(j, half):
            at = ys[j]
            return wt.at[hi(at), 0, hi(xs[k]), lo(xs[k]), lo(at), half_rows(half)]

        def part_b(j, half):
            at = xs[j]
            return wt.at[hi(ys[k]), 1, hi(at), lo(at), lo(ys[k]), half_rows(half)]

        part, right, left = ((part_a, yr, yd), (part_b, xr, xl))[axis]
        return Reduce(part, right, left, ra.at[axis, k], ta.at[axis, k])

    def second_stage(axis):
        def part(j, half):
            return r1.at[axis, j, half_rows(half)]

        right, left = ((xr, xl), (yr, yd))[axis]
        return Reduce(part, right, left, rc.at[axis], tc.at[axis])

    stage1 = [[first_stage(axis, k) for k in range(4)] for axis in range(2)]
    stage2 = [second_stage(axis) for axis in range(2)]

    def begin(k):
        for axis in range(2):
            stage1[axis][k].far()
            stage1[axis][k].near()

    def chain(k):
        for axis in range(2):
            stage1[axis][k].chain()

    def finish(k):
        for axis in range(2):
            for half, value in enumerate(stage1[axis][k].finish()):
                r1[axis, k, half_rows(half), :] = value.astype(BF)

    ways = (
        (((4, 0), (3, 1), (3, 0), (2, 1), (2, 0), (1, 1), (1, 0)), 1, zr),
        (((4, 1), (3, 0), (3, 1), (2, 0), (2, 1), (1, 0), (1, 1)), -1, zl),
    )
    flying = {}

    def hop(order):
        for d, (way, sign, to) in enumerate(ways):
            distance, half = way[order]
            offset = sign * distance if distance < 4 else 4
            rows = slice(half * 128, half * 128 + 128)
            value = total_of(offsets.index(offset), rows)
            before = (distance + 1, half)
            if before in way:
                prior = way.index(before)
                flying[d, prior].wait_recv()
                value = value + cr[d, prior].astype(F32)
            cs[d, order] = value.astype(BF)
            flying[d, order] = copy(cs.at[d, order], cr.at[d, order], to)

    def met(*indices):
        for i in indices:
            across[i].wait_recv()

    grads(lambda i: (i, 0, 1 - xh))
    stage1[0][2].far()
    stage1[0][2].near()
    grads(lambda i: (1 - yh, 1, i))
    stage1[1][2].far()
    stage1[1][2].near()
    across += [input_grad(1), input_grad(2)]
    met(0)
    hop(0)
    grads(lambda i: (i, 0, xh))
    grads(lambda i: (yh, 1, i))
    begin(1)
    begin(3)
    met(1, 2)
    hop(1)
    chain(2)
    across += [input_grad(i) for i in range(3, 8)]
    begin(0)
    chain(1)
    chain(3)
    met(3, 4)
    hop(2)

    for s in range(2):
        prod = jnp.zeros((256, HS), F32)
        for a in range(3):
            prod = prod + gb[1 + a, s].astype(F32) * sb[a, s].astype(F32)
        ts[s] = jnp.broadcast_to(jnp.sum(prod.T, axis=0, keepdims=True), (8, 256))
    inner_pair = copy(ts.at[other], tr, sibling)

    finish(2)
    for axis in range(2):
        stage2[axis].far()
    hop(3)
    chain(0)
    inner_pair.wait_recv()
    tl[...] = ts[core] + tr[...]
    tt[mp] = tl[...]
    inner = [copy(tl, tt.at[mp], along_z(k)) for k in range(1, 8)]
    met(5, 6, 7)
    hop(4)
    finish(1)
    finish(3)
    for axis in range(2):
        stage2[axis].near()
    hop(5)
    for axis in range(2):
        stage2[axis].chain()
    hop(6)
    finish(0)
    for axis in range(2):
        for half, value in enumerate(stage2[axis].finish()):
            rf[axis, half_rows(half), :] = value
    fs[...] = rf[other].astype(BF)
    last = copy(fs, fr, sibling)
    fh[core] = rf[core]

    for c in inner:
        c.wait_recv()
    inner_row = tt[0]
    for k in range(1, 8):
        inner_row = inner_row + tt[k]
    inner_col = jnp.broadcast_to(inner_row[0:1, :] / 4096.0, (HS, 256)).T
    for d in range(2):
        for order in (5, 6):
            flying[d, order].wait_recv()
    for half in range(2):
        rows = slice(half * 128, half * 128 + 128)
        grad = total_of(7, rows)
        for d, (way, _, _) in enumerate(ways):
            grad = grad + cr[d, way.index((1, half))].astype(F32)
        inverse = iv[rows, :]
        back = inverse * inverse * inner_col[rows, :]
        for g in range(4):
            cols = slice(g * HS, (g + 1) * HS)
            scaled = grad[:, cols] * gain[:, cols]
            branch = inverse * scaled - xs_in[rows, cols].astype(F32) * back
            value = (dy[mp, core, rows, cols].astype(F32) + branch).astype(BF)
            for j in range(2):
                span_v[j, rows, cols] = jnp.where(which == j, value, jnp.zeros_like(value))
    written = [fetch(span_v, span_out.at[0])]

    last.wait_recv()
    fh[other] = fr[...].astype(F32)
    for h in range(2):
        cols = slice(h * HS, (h + 1) * HS)
        for a in range(3):
            g_v[a, :, cols] = fh[h, a * HS : (a + 1) * HS, :].T
        o_v[cols, :] = fh[h, 3 * HS :, :]
    for a, ref in enumerate((q_out, k_out, v_out)):
        written.append(fetch(g_v.at[a], ref))
    written.append(fetch(o_v, o_out))
    for c in copy.started:
        c.wait_send()
    for c in written:
        c.wait()


def hand_over(*refs):
    for src, dst in zip(refs[:5], refs[5:]):
        dst[...] = src[...]


def local(spans, frame_span, norm_gain, w_query, w_key, w_value, w_out, grad_out):
    vmem = pl.BlockSpec(memory_space=pltpu.VMEM)
    smem = pl.BlockSpec(memory_space=pltpu.SMEM)
    anywhere = pl.BlockSpec(memory_space=pl.ANY)
    shape = jax.ShapeDtypeStruct
    scratch = [
        ((2, 256, 512), BF),
        ((256, 512), BF),
        ((8, 2, 256, 512), BF),
        ((8, 2, 256, 512), BF),
        ((3, 128, 256), BF),
        ((256, 128), BF),
        ((2, 128, 512), BF),
        ((2, 2, 2, 2, 2, 128, 512), BF),
        ((8, 8, 256), F32),
        ((8, 256), F32),
        ((256, 128), F32),
        ((2, 256, 384), F32),
        ((2, 256, 128), F32),
        ((4, 2, 256, 128), BF),
        ((4, 2, 8, 32, 128), BF),
        ((2, 256, 256), F32),
        ((2, 256, 256), BF),
        ((4, 2, 8, 32, 128), BF),
        ((4, 2, 256, 128), BF),
        ((2, 256, 384), BF),
        ((512, 512), BF),
        ((2, 8, 256), F32),
        ((8, 256), F32),
        ((8, 256), F32),
        ((8, 8, 256), F32),
        ((8, 256, 512), BF),
        ((8, 256, 512), BF),
        ((8, 256, 512), F32),
        ((2, 7, 128, 512), BF),
        ((2, 7, 128, 512), BF),
        ((2, 2, 2, 2, 2, 512, 128), BF),
        ((2, 4, 6, 256, 128), BF),
        ((2, 4, 2, 256, 128), BF),
        ((2, 4, 512, 128), BF),
        ((2, 6, 256, 128), BF),
        ((2, 2, 256, 128), BF),
        ((2, 512, 128), F32),
        ((512, 128), BF),
        ((512, 128), BF),
        ((2, 512, 128), F32),
        ((2, 256, 512), BF),
        ((3, 128, 256), F32),
        ((256, 128), F32),
    ]
    out_shape = (
        shape((1, 2, 256, 512), BF),
        shape((128, 256), F32),
        shape((128, 256), F32),
        shape((128, 256), F32),
        shape((256, 128), F32),
    )
    results = pl.pallas_call(
        kernel,
        out_shape=out_shape,
        in_specs=[anywhere, smem, vmem] + [anywhere] * 5,
        out_specs=(anywhere,) * 5,
        scratch_shapes=[pltpu.VMEM(*each) for each in scratch]
        + [pltpu.SemaphoreType.DMA((n,)) for n in (COPIES, COPIES, 16)],
        compiler_params=pltpu.CompilerParams(
            collective_id=0, has_side_effects=True, vmem_limit_bytes=56 * 1024 * 1024
        ),
    )(spans, frame_span, norm_gain[None, :], w_query, w_key, w_value, w_out, grad_out)
    return pl.pallas_call(
        hand_over,
        out_shape=out_shape,
        in_specs=[vmem] * 5,
        out_specs=(vmem,) * 5,
    )(*results)


def solution(mesh):
    placed = (
        P("dp", "tm", None, "mp"),
        P("dp", "tm"),
        P("mp"),
        P(("dp", "tm"), "mp"),
        P(("dp", "tm"), "mp"),
        P(("dp", "tm"), "mp"),
        P("mp", ("dp", "tm")),
        P("dp", "tm", None, "mp"),
    )
    return jax.shard_map(
        local,
        mesh=mesh,
        in_specs=placed,
        out_specs=(
            P("dp", "tm", None, "mp"),
            P(("dp", "tm"), "mp"),
            P(("dp", "tm"), "mp"),
            P(("dp", "tm"), "mp"),
            P("mp", ("dp", "tm")),
        ),
        check_vma=False,
    )
```

```python
import math

import jax
import jax.numpy as jnp
from jax import lax
from jax.experimental import pallas as pl
from jax.experimental.pallas import tpu as pltpu
from jax.sharding import PartitionSpec as P

HS = 128
EPSILON = 1e-05
BF = jnp.bfloat16
F32 = jnp.float32
MESH = pl.DeviceIdType.MESH
ARRIVALS = 100
DEPARTURES = 8
RULER = 6144

ROWS_COLS = (((1,), (1,)), ((), ()))


def dot(left, right):
    return jnp.dot(left, right, preferred_element_type=F32)


def dot_t(left, right):
    return lax.dot_general(left, right, ROWS_COLS, preferred_element_type=F32)


class Batch:
    def __init__(self, copies, at):
        self.copies = copies
        self.at = at
        self.kib = 0

    def __call__(self, src, dst, device):
        copies = self.copies
        kib = math.prod(dst.shape) * jnp.dtype(dst.dtype).itemsize // 1024
        if copies.departed[-1] + kib > RULER:
            copies.departed.append(0)
        copies.departed[-1] += kib
        self.kib += kib
        pltpu.make_async_remote_copy(
            src_ref=src,
            dst_ref=dst,
            send_sem=copies.send.at[len(copies.departed) - 1],
            recv_sem=copies.recv.at[self.at],
            device_id=device,
            device_id_type=MESH,
        ).start()

    def wait(self):
        copies = self.copies
        copies.open.remove(self)
        copies.wait(copies.recv.at[self.at], self.kib)


class Copies:
    def __init__(self, send, recv, ruler):
        self.send = send
        self.recv = recv
        self.ruler = ruler
        self.departed = [0]
        self.count = 0
        self.open = []

    def batch(self):
        assert self.count < ARRIVALS
        new = Batch(self, self.count)
        self.count += 1
        self.open.append(new)
        return new

    def __call__(self, src, dst, device):
        new = self.batch()
        new(src, dst, device)
        return new

    def wait(self, sem, kib):
        span = self.ruler.at[pl.ds(0, kib)]
        pltpu.make_async_copy(span, span, sem).wait()

    def finish(self):
        assert not self.open
        assert len(self.departed) <= DEPARTURES
        for at, kib in enumerate(self.departed):
            self.wait(self.send.at[at], kib)


def kernel(
    spans_ref,
    which_ref,
    gain_ref,
    wq_ref,
    wk_ref,
    wv_ref,
    wo_ref,
    dy_ref,
    span_out,
    q_out,
    k_out,
    v_out,
    o_out,
    sp,
    xs_in,
    xn,
    dy,
    wl,
    wol,
    wp,
    wg,
    ss,
    sl,
    iv,
    aq,
    aa,
    sb,
    rb,
    so,
    st,
    ob,
    gb,
    gc,
    gt,
    ts,
    tr,
    tl,
    tt,
    ps,
    sr,
    cs,
    cr,
    wt,
    wt_o,
    ra_o,
    ta_o,
    r1_o,
    rc_o,
    tc_o,
    ra,
    ta,
    r1,
    rc,
    tc,
    rf,
    fs,
    fr,
    fh,
    span_v,
    g_v,
    o_v,
    ruler,
    send,
    recv,
    near_sem,
):
    dp = lax.axis_index("dp")
    tm = lax.axis_index("tm")
    mp = lax.axis_index("mp")
    core = lax.rem(dp, 2)
    other = 1 - core
    yh = lax.div(dp, 2)
    x = lax.div(tm, 2)
    yl = lax.rem(tm, 2)
    y = yh * 2 + yl

    def hi(v):
        return lax.div(v, 2)

    def lo(v):
        return lax.rem(v, 2)

    def device(x_at, y_at):
        return (hi(y_at) * 2 + core, x_at * 2 + lo(y_at), mp)

    def ring8(offset):
        return lax.rem(mp + offset + 8, 8)

    def along_z(offset):
        return (dp, tm, ring8(offset))

    def along_tm(offset):
        return (dp, lax.rem(tm + offset, 8), mp)

    sibling = (yh * 2 + other, tm, mp)
    zr, zl = along_z(1), along_z(-1)
    xs = tuple(lax.rem(x + k, 4) for k in range(4))
    ys = tuple(lax.rem(y + k, 4) for k in range(4))
    xh = hi(x)
    xr, xl = device(xs[1], y), device(xs[3], y)
    yr, yd = device(x, ys[1]), device(x, ys[3])
    far_y = device(x, lax.rem(y + 3 + 2 * yl, 4))

    barrier = pltpu.get_barrier_semaphore()
    partners = [sibling, far_y]
    partners += [along_z(k) for k in range(1, 8)]
    partners += [along_tm(k) for k in range(1, 8)]
    for partner in partners:
        pl.semaphore_signal(barrier, inc=1, device_id=partner, device_id_type=MESH)

    fetched = []

    def fetch(src, dst):
        c = pltpu.make_async_copy(src, dst, near_sem.at[len(fetched)])
        c.start()
        fetched.append(c)
        return c

    span_in = fetch(spans_ref.at[0], sp)
    w_in = [fetch(ref, wl.at[a]) for a, ref in enumerate((wq_ref, wk_ref, wv_ref))]
    w_in.append(fetch(wo_ref, wol))
    dy_in = fetch(dy_ref.at[0, 0], dy.at[mp, core])

    which = which_ref[0, 0]
    gain = gain_ref[...].astype(F32).reshape(1, 512)
    span_in.wait()
    xs_in[...] = jnp.where(which == 0, sp[0], sp[1])
    sums = jnp.zeros((256, HS), F32)
    for g in range(4):
        part = xs_in[:, g * HS : (g + 1) * HS].astype(F32)
        sums = sums + part * part
    row = jnp.sum(sums.T, axis=0, keepdims=True)
    sl[...] = jnp.broadcast_to(row, (8, 256))
    for c in w_in:
        c.wait()
    for h in range(2):
        for a in range(3):
            wp[h, :, a * HS : (a + 1) * HS] = wl[a, :, h * HS : (h + 1) * HS]
        wp[h, :, 3 * HS :] = wol[h * HS : (h + 1) * HS, :].astype(F32).T.astype(BF)
    pl.semaphore_wait(barrier, len(partners))

    copy = Copies(send, recv, ruler)

    halves = (
        ((1, 0, 128), (1, 128, 128), (2, 0, 128), (2, 128, 128), (3, 0, 128), (3, 128, 128), (4, 0, 128)),
        ((1, 128, 128), (1, 0, 128), (2, 128, 128), (2, 0, 128), (3, 128, 128), (3, 0, 128), (4, 128, 128)),
    )
    first_half = ((1, 0, 128), (1, 128, 128), (2, 0, 128), (3, 0, 128))
    staged = (
        first_half
        + ((4, 0, 64), (2, 128, 64), (2, 192, 64))
        + ((3, 128, 64), (3, 192, 64), (4, 128, 64)),
        first_half
        + ((4, 64, 64), (2, 192, 64), (2, 128, 64))
        + ((3, 192, 64), (3, 128, 64), (4, 192, 64)),
    )

    class Ring:
        def __init__(self, ref, ways, src):
            self.ref = ref
            self.ways = ways
            self.src = src
            self.flight = {}
            self.pending = {}

        def part(self, d, k, first, rows):
            offset = -k if d == 0 else k
            return self.ref.at[ring8(offset), core, pl.ds(first, rows)]

        def pass_on(self, d, j):
            k, first, rows = self.ways[d][j]
            part = self.part(d, k - 1, first, rows)
            src = self.src.at[pl.ds(first, rows)] if k == 1 else part
            if d == 0:
                self.flight[j] = copy.batch()
            self.flight[j](src, part, (zr, zl)[d])

        def send(self, *which_parts):
            for j in which_parts:
                for d in range(2):
                    self.pass_on(d, j)

        def take(self, *which_parts, then=()):
            for at, j in enumerate(which_parts):
                self.flight[j].wait()
                if then:
                    self.send(then[at])

        def share(self, *which_parts, half=0):
            for d in range(2):
                rows = [self.ways[d][j] for j in which_parts]
                first = min(r[1] for r in rows)
                part = self.part(d, rows[0][0], first, sum(r[2] for r in rows))
                self.hand(part, half)

        def hand(self, part, half=0):
            if half not in self.pending:
                self.pending[half] = copy.batch()
            self.pending[half](part, part, sibling)

        def settle(self, half=0):
            if half in self.pending:
                self.pending.pop(half).wait()

    grad_in = dy_ref.at[0, 0]
    ring_dy = Ring(dy, staged, grad_in)
    sumsq = copy.batch()
    for k in range(1, 8):
        sumsq(sl, ss.at[mp], along_z(k))
    ss[mp] = sl[...]
    mine = wg.at[yh, core, xh, lo(x), yl]
    pair = copy(wp.at[other], mine, sibling)
    ring_dy.send(0, 1)
    wg[yh, core, xh, lo(x), yl] = wp[core]

    class Spread:
        def __init__(self, at, ring, right, left):
            self.at = at
            self.ring = ring
            self.to = (right, left)
            own = at(ring[0])
            self.trip = copy.batch()
            self.trip(own, own, right)
            self.trip(own, own, left)

        def relay(self):
            self.trip.wait()
            self.trip = copy.batch()
            part = self.at(self.ring[3]).at[pl.ds(0, 64)]
            self.trip(part, part, self.to[0])
            part = self.at(self.ring[1]).at[pl.ds(64, 64)]
            self.trip(part, part, self.to[1])

        def done(self):
            self.trip.wait()

    def block(x_at, y_at, s):
        return wg.at[hi(y_at), s, hi(x_at), lo(x_at), lo(y_at)]

    def spread_a(k):
        return Spread(lambda v: block(xs[k], v, 0), ys, yr, yd)

    def spread_b(k):
        return Spread(lambda v: block(v, ys[k], 1), xs, xr, xl)

    pair.wait()
    a1 = Spread(lambda v: block(v, y, 0), xs, xr, xl)
    b1 = Spread(lambda v: block(x, v, 1), ys, yr, yd)
    second = {0: (spread_a(0), spread_b(0))}

    sumsq.wait()
    total = ss[0]
    for k in range(1, 8):
        total = total + ss[k]
    inv_row = lax.rsqrt(total / 4096.0 + EPSILON)
    iv[...] = jnp.broadcast_to(inv_row[0:1, :], (HS, 256)).T
    for g in range(4):
        cols = slice(g * HS, (g + 1) * HS)
        xn[mp, core, :, cols] = (
            xs_in[:, cols].astype(F32) * iv[...] * gain[:, cols]
        ).astype(BF)
    ring_xn = Ring(xn, halves, xn.at[mp, core])
    ring_xn.send(0, 1)
    ring_xn.hand(xn.at[mp, core])
    ring_dy.take(0, then=(2,))
    aq[...] = jnp.zeros_like(aq)
    aa[...] = jnp.zeros_like(aa)

    a1.relay()
    b1.relay()
    for k in (3, 1):
        second[k] = (spread_a(k), spread_b(k))

    def relay(k):
        second[k][0].relay()
        second[k][1].relay()

    relay(0)
    dy_in.wait()
    ring_dy.hand(dy.at[mp, core, pl.ds(0, 128)], 0)
    ring_dy.hand(dy.at[mp, core, pl.ds(128, 128)], 1)
    ring_dy.take(1)
    ring_dy.share(0)
    ring_dy.share(1, half=1)
    a1.done()
    b1.done()
    second[2] = (spread_a(2), spread_b(2))
    ring_xn.take(0, then=(2,))
    ring_xn.take(1, then=(3,))
    ring_xn.share(0, 1)
    relay(3)
    ring_dy.take(2, then=(3,))
    ring_dy.share(2)
    relay(1)
    ring_xn.take(2, then=(4,))
    relay(2)
    ring_xn.take(3, then=(5,))
    ring_xn.share(2, 3)
    ring_dy.take(3, then=(4,))
    ring_dy.share(3)
    for k in range(4):
        second[k][0].done()
        second[k][1].done()

    def weights(m, cols):
        return wg[lax.div(m, 4), lo(hi(m)), lo(m), :, :, :, cols].reshape(512, -1)

    qkv_cols = slice(0, 3 * HS)
    out_cols = slice(3 * HS, 4 * HS)

    def forward(ref, into, cols, rows, first, step, count):
        def body(i, carry):
            m = ring8(first + step * i)
            shape = (2, rows.stop - rows.start)
            left = ref[m, :, rows].reshape(shape[0] * shape[1], 512)
            into[:, rows] += dot(left, weights(m, cols)).reshape(*shape, -1)
            return carry

        lax.fori_loop(0, count, body, 0)

    def forward_xn(*which_chunks):
        ring_xn.settle()
        forward(xn, aq, qkv_cols, slice(0, 256), *which_chunks)

    def group(half):
        return slice(half * 128, half * 128 + 128)

    def forward_dy(half, *which_chunks):
        ring_dy.settle(half)
        forward(dy, aa, out_cols, group(half), *which_chunks)

    forward_xn(-1, 1, 3)
    ring_xn.take(4, then=(6,))
    ring_dy.send(5, 6)
    forward_dy(0, -1, 1, 3)
    ring_xn.take(5)
    ring_xn.share(4, 5)
    forward_xn(-2, 4, 2)
    ring_dy.take(4)
    ring_dy.hand(dy.at[ring8(4), core, pl.ds(0, 128)])
    forward_dy(0, -2, 4, 2)
    forward_dy(0, -3, 6, 2)
    forward_xn(-3, 6, 2)
    ring_xn.take(6)
    ring_xn.hand(xn.at[ring8(4), core])
    forward_dy(0, 4, 0, 1)

    def strip(at):
        return pl.ds(pl.multiple_of(at * 16, 16), 16)

    def swap_out(arrays, parts):
        trips = copy.batch()
        for k in range(1, 8):
            src = sb.at[arrays, parts, :, strip(lax.rem(tm + k, 8))]
            trips(src, rb.at[arrays, parts, :, tm], along_tm(k))
        rb[arrays, parts, :, tm] = sb[arrays, parts, :, strip(tm), :]
        return trips

    def swap_back(arrays, parts):
        trips = copy.batch()
        for k in range(1, 8):
            dst = gb.at[arrays, parts, :, strip(tm)]
            trips(ob.at[arrays, parts, :, lax.rem(tm + k, 8)], dst, along_tm(k))
        gb[arrays, parts, :, strip(tm), :] = ob[arrays, parts, :, tm]
        return trips

    both = pl.ds(0, 2)
    one = (pl.ds(0, 1), pl.ds(1, 1))

    def grads_out(part):
        for s in range(2):
            sb[3, part, s] = aa[s, group(part)].astype(BF)
        return swap_out(pl.ds(3, 1), one[part])

    away = [grads_out(0)]
    forward_xn(4, 0, 1)
    ring_dy.take(5, then=(7,))
    for s in range(2):
        for a in range(3):
            for part in range(2):
                sb[a, part, s] = aq[s, group(part), a * HS : (a + 1) * HS].astype(BF)
    trips = swap_out(pl.ds(0, 3), both)
    ring_dy.take(6, then=(8,))
    ring_dy.share(5, 6, half=1)
    forward_dy(1, -1, 1, 3)
    ring_dy.take(7, then=(9,))
    forward_dy(1, -2, 4, 2)
    ring_dy.take(8)
    ring_dy.share(7, 8, half=1)
    forward_dy(1, -3, 6, 2)
    ring_dy.take(9)
    ring_dy.hand(dy.at[ring8(4), core, pl.ds(128, 128)], 1)
    forward_dy(1, 4, 0, 1)
    away.append(grads_out(1))
    trips.wait()

    row_id = lax.broadcasted_iota(jnp.int32, (256, 256), 0)
    col_id = lax.broadcasted_iota(jnp.int32, (256, 256), 1)
    same = ((row_id & 15) == (col_id & 15)) & ((row_id >> 7) == (col_id >> 7))
    seen = same & ((row_id >> 4) >= (col_id >> 4))
    scale = HS ** (-0.5)

    def held(i, part):
        return rb[i, part].reshape(256, HS)

    def attend(part):
        q, k, v = (held(i, part) for i in range(3))
        scores = jnp.where(seen, dot_t(q, k) * scale, -1e30)
        expo = jnp.exp(scores - jnp.max(scores, axis=1, keepdims=True))
        soft = expo / jnp.sum(expo, axis=1, keepdims=True)
        so[part] = soft
        st[part] = soft.T.astype(BF)
        ob[0, part] = dot(soft.astype(BF), v).astype(BF).reshape(2, 8, 16, HS)

    def attend_back(part):
        away[part].wait()
        q, k, v, a = (held(i, part) for i in range(4))
        soft = so[part]
        dsoft = dot_t(a, v)
        dscore = soft * (dsoft - jnp.sum(dsoft * soft, axis=1, keepdims=True)) * scale
        results = (
            dot(dscore.astype(BF), k),
            dot(dscore.T.astype(BF), q),
            dot(st[part], a),
        )
        for i, value in enumerate(results):
            ob[1 + i, part] = value.astype(BF).reshape(2, 8, 16, HS)
        return swap_back(pl.ds(1, 3), one[part])

    attend(0)
    back = [attend_back(0)]
    attend(1)
    att_trips = swap_back(pl.ds(0, 1), both)
    back.append(attend_back(1))

    def keep_transposed(a):
        for part in range(2):
            for s in range(2):
                first = s * 256 + part * 128
                source = gb[(a + 1) % 4, part, s].astype(F32)
                gt[a * HS : (a + 1) * HS, first : first + 128] = source.T.astype(BF)

    def out_grad(m, carry):
        value = dot(gt[3 * HS :, :], dy[m].reshape(512, 512)).astype(BF)
        place = wt_o.at[lax.div(m, 4), lo(hi(m)), lo(m)]
        for i in range(4):
            place[i // 2, i % 2] = value[:, i * HS : (i + 1) * HS]
        return carry

    att_trips.wait()
    keep_transposed(3)
    lax.fori_loop(0, 8, out_grad, 0)

    offsets = (4, 3, -3, 2, -2, 1, -1, 0)

    def grads_in(half):
        for s in range(2):
            for a in range(3):
                gc[s, group(half), a * HS : (a + 1) * HS] = gb[1 + a, half, s]

    def input_grads(half, first, last):
        met = copy.batch()
        rows = group(half)
        for index in range(first, last):
            w = weights(ring8(offsets[index]), qkv_cols)
            value = dot_t(gc[:, rows, :].reshape(256, 3 * HS), w).astype(BF)
            ps[index, :, rows, :] = value.reshape(2, 128, 512)
            part = pl.ds(half * 128, 128)
            met(ps.at[index, other, part], sr.at[index, part], sibling)
        across.append(met)

    across = []

    def total_of(index, half):
        rows = group(half)
        return ps[index, core, rows, :].astype(F32) + sr[index, rows, :].astype(F32)

    ways = (((4, 3, 2, 1), (3, 2, 1)), ((3, 2, 1), (4, 3, 2, 1)))
    flying = {}

    def hop(half, order):
        if across and order < 2:
            across.pop().wait()
        if order:
            flying[half].wait()
        flying[half] = copy.batch()
        slot = half * 4 + order
        for d in range(2):
            way = ways[half][d]
            if order >= len(way):
                continue
            distance = way[order]
            offset = 4 if distance == 4 else (distance, -distance)[d]
            value = total_of(offsets.index(offset), half)
            if order:
                value = value + cr[d, slot - 1].astype(F32)
            cs[d, slot] = value.astype(BF)
            flying[half](cs.at[d, slot], cr.at[d, slot], (zr, zl)[d])

    class Reduce:
        def __init__(self, part, right, left, got, tmp):
            self.part = part
            self.to = (right, left)
            self.got = got
            self.tmp = tmp

        def far(self):
            self.first = copy.batch()
            self.first(self.part(2, 0), self.got.at[0], self.to[0])
            self.first(self.part(2, 1), self.got.at[1], self.to[1])

        def near(self):
            self.second = copy.batch()
            self.second(self.part(1, 1), self.got.at[2], self.to[0])
            self.second(self.part(3, 0), self.got.at[3], self.to[1])

        def chain(self):
            self.first.wait()
            for d, (at, half) in enumerate(((1, 0), (3, 1))):
                value = self.part(at, half)[...].astype(F32) + self.got[d].astype(F32)
                self.tmp[d] = value.astype(BF)
                self.second(self.tmp.at[d], self.got.at[4 + d], self.to[d])

        def finish(self):
            got = self.got
            self.second.wait()
            first = self.part(0, 0)[...].astype(F32) + got[3].astype(F32) + got[4].astype(F32)
            second = self.part(0, 1)[...].astype(F32) + got[2].astype(F32) + got[5].astype(F32)
            return first, second

    def out_first(axis):
        def part_a(j, half):
            return wt_o.at[hi(ys[j]), 0, half, :, lo(ys[j])]

        def part_b(j, half):
            return wt_o.at[half, 1, hi(xs[j]), lo(xs[j]), :]

        part, right, left = ((part_a, yr, yd), (part_b, xr, xl))[axis]
        return Reduce(part, right, left, ra_o.at[axis], ta_o.at[axis])

    def out_second(axis):
        ring = (xs, ys)[axis]

        def part(j, half):
            return r1_o.at[axis, hi(ring[j]), lo(ring[j]), pl.ds(half * 64, 64)]

        right, left = ((xr, xl), (yr, yd))[axis]
        return Reduce(part, right, left, rc_o.at[axis], tc_o.at[axis])

    out1 = [out_first(axis) for axis in range(2)]
    out2 = [out_second(axis) for axis in range(2)]
    for stage in out1:
        stage.far()
        stage.near()
    back[0].wait()
    grads_in(0)
    input_grads(0, 0, 3)
    back[1].wait()

    for a in range(3):
        keep_transposed(a)

    def weight_grad(yh_at, s_at, xh_at):
        m = (yh_at * 2 + s_at) * 2 + xh_at
        value = dot(gt[: 3 * HS, :], xn[m].reshape(512, 512)).astype(BF)
        for i in range(4):
            wt[yh_at, s_at, xh_at, i // 2, i % 2] = value[:, i * HS : (i + 1) * HS]

    def grads(which_chunk):
        def body(i, carry):
            weight_grad(*which_chunk(i))
            return carry

        lax.fori_loop(0, 2, body, 0)

    def half_rows(half):
        return slice(half * 192, half * 192 + 192)

    def first_stage(axis, k):
        def part_a(j, half):
            at = ys[j]
            return wt.at[hi(at), 0, hi(xs[k]), lo(xs[k]), lo(at), half_rows(half)]

        def part_b(j, half):
            at = xs[j]
            return wt.at[hi(ys[k]), 1, hi(at), lo(at), lo(ys[k]), half_rows(half)]

        part, right, left = ((part_a, yr, yd), (part_b, xr, xl))[axis]
        return Reduce(part, right, left, ra.at[axis, k], ta.at[axis, k])

    def second_stage(axis):
        def part(j, half):
            return r1.at[axis, j, half_rows(half)]

        right, left = ((xr, xl), (yr, yd))[axis]
        return Reduce(part, right, left, rc.at[axis], tc.at[axis])

    stage1 = [[first_stage(axis, k) for k in range(4)] for axis in range(2)]
    stage2 = [second_stage(axis) for axis in range(2)]

    def begin(k):
        for axis in range(2):
            stage1[axis][k].far()
            stage1[axis][k].near()

    def chain(k):
        for axis in range(2):
            stage1[axis][k].chain()

    def finish(k):
        for axis in range(2):
            for half, value in enumerate(stage1[axis][k].finish()):
                r1[axis, k, half_rows(half), :] = value.astype(BF)

    grads(lambda i: (i, 0, 1 - xh))
    stage1[0][2].far()
    stage1[0][2].near()
    hop(0, 0)
    grads(lambda i: (1 - yh, 1, i))
    stage1[1][2].far()
    stage1[1][2].near()
    grads_in(1)
    input_grads(1, 0, 3)
    grads(lambda i: (i, 0, xh))
    for k in (1, 3):
        stage1[0][k].far()
        stage1[0][k].near()
    hop(1, 0)
    grads(lambda i: (yh, 1, i))
    for k in (1, 3):
        stage1[1][k].far()
        stage1[1][k].near()
    input_grads(0, 3, 8)
    chain(2)
    hop(0, 1)
    begin(0)
    for stage in out1:
        stage.chain()
    input_grads(1, 3, 8)
    chain(1)
    chain(3)
    hop(1, 1)
    finish(2)
    for axis in range(2):
        stage2[axis].far()
    hop(0, 2)
    for axis in range(2):
        for half, value in enumerate(out1[axis].finish()):
            r1_o[axis, half] = value.astype(BF)
        out2[axis].far()
        out2[axis].near()
    chain(0)

    for s in range(2):
        prod = jnp.zeros((256, HS), F32)
        for a in range(3):
            left = jnp.concatenate([gb[1 + a, part, s] for part in range(2)], axis=0)
            right = jnp.concatenate([sb[a, part, s] for part in range(2)], axis=0)
            prod = prod + left.astype(F32) * right.astype(F32)
        ts[s] = jnp.broadcast_to(jnp.sum(prod.T, axis=0, keepdims=True), (8, 256))
    inner_pair = copy(ts.at[other], tr, sibling)

    hop(1, 2)
    for stage in out2:
        stage.chain()
    finish(1)
    finish(3)
    for axis in range(2):
        stage2[axis].near()
    inner_pair.wait()
    tl[...] = ts[core] + tr[...]
    tt[mp] = tl[...]
    inner = copy.batch()
    for k in range(1, 8):
        inner(tl, tt.at[mp], along_z(k))
    hop(0, 3)
    for axis in range(2):
        stage2[axis].chain()
    hop(1, 3)
    finish(0)
    for axis in range(2):
        for half, value in enumerate(out2[axis].finish()):
            rf[axis, 384 + half * 64 : 448 + half * 64, :] = value
        for half, value in enumerate(stage2[axis].finish()):
            rf[axis, half_rows(half), :] = value
    fs[...] = rf[other].astype(BF)
    last = copy(fs, fr, sibling)
    fh[core] = rf[core]

    inner.wait()
    inner_row = tt[0]
    for k in range(1, 8):
        inner_row = inner_row + tt[k]
    inner_col = jnp.broadcast_to(inner_row[0:1, :] / 4096.0, (HS, 256)).T
    for half in range(2):
        rows = group(half)
        flying[half].wait()
        grad = total_of(7, half)
        for d in range(2):
            final = len(ways[half][d]) - 1
            grad = grad + cr[d, half * 4 + final].astype(F32)
        inverse = iv[rows, :]
        back = inverse * inverse * inner_col[rows, :]
        for g in range(4):
            cols = slice(g * HS, (g + 1) * HS)
            scaled = grad[:, cols] * gain[:, cols]
            branch = inverse * scaled - xs_in[rows, cols].astype(F32) * back
            value = (dy[mp, core, rows, cols].astype(F32) + branch).astype(BF)
            for j in range(2):
                span_v[j, rows, cols] = jnp.where(which == j, value, jnp.zeros_like(value))
    written = [fetch(span_v, span_out.at[0])]

    last.wait()
    fh[other] = fr[...].astype(F32)
    for h in range(2):
        cols = slice(h * HS, (h + 1) * HS)
        for a in range(3):
            g_v[a, :, cols] = fh[h, a * HS : (a + 1) * HS, :].T
        o_v[cols, :] = fh[h, 3 * HS :, :]
    for a, ref in enumerate((q_out, k_out, v_out)):
        written.append(fetch(g_v.at[a], ref))
    written.append(fetch(o_v, o_out))
    copy.finish()
    for c in written:
        c.wait()


def hand_over(*refs):
    for src, dst in zip(refs[:5], refs[5:]):
        dst[...] = src[...]


def local(spans, frame_span, norm_gain, w_query, w_key, w_value, w_out, grad_out):
    vmem = pl.BlockSpec(memory_space=pltpu.VMEM)
    smem = pl.BlockSpec(memory_space=pltpu.SMEM)
    anywhere = pl.BlockSpec(memory_space=pl.ANY)
    shape = jax.ShapeDtypeStruct
    scratch = [
        ((2, 256, 512), BF),
        ((256, 512), BF),
        ((8, 2, 256, 512), BF),
        ((8, 2, 256, 512), BF),
        ((3, 128, 256), BF),
        ((256, 128), BF),
        ((2, 128, 512), BF),
        ((2, 2, 2, 2, 2, 128, 512), BF),
        ((8, 8, 256), F32),
        ((8, 256), F32),
        ((256, 128), F32),
        ((2, 256, 384), F32),
        ((2, 256, 128), F32),
        ((4, 2, 2, 128, 128), BF),
        ((4, 2, 2, 8, 16, 128), BF),
        ((2, 256, 256), F32),
        ((2, 256, 256), BF),
        ((4, 2, 2, 8, 16, 128), BF),
        ((4, 2, 2, 128, 128), BF),
        ((2, 256, 384), BF),
        ((512, 512), BF),
        ((2, 8, 256), F32),
        ((8, 256), F32),
        ((8, 256), F32),
        ((8, 8, 256), F32),
        ((8, 2, 256, 512), BF),
        ((8, 256, 512), BF),
        ((2, 8, 128, 512), BF),
        ((2, 8, 128, 512), BF),
        ((2, 2, 2, 2, 2, 384, 128), BF),
        ((2, 2, 2, 2, 2, 128, 128), BF),
        ((2, 6, 2, 128, 128), BF),
        ((2, 2, 2, 128, 128), BF),
        ((2, 2, 2, 128, 128), BF),
        ((2, 6, 64, 128), BF),
        ((2, 2, 64, 128), BF),
        ((2, 4, 6, 192, 128), BF),
        ((2, 4, 2, 192, 128), BF),
        ((2, 4, 384, 128), BF),
        ((2, 6, 192, 128), BF),
        ((2, 2, 192, 128), BF),
        ((2, 512, 128), F32),
        ((512, 128), BF),
        ((512, 128), BF),
        ((2, 512, 128), F32),
        ((2, 256, 512), BF),
        ((3, 128, 256), F32),
        ((256, 128), F32),
        ((RULER, 256), F32),
    ]
    out_shape = (
        shape((1, 2, 256, 512), BF),
        shape((128, 256), F32),
        shape((128, 256), F32),
        shape((128, 256), F32),
        shape((256, 128), F32),
    )
    results = pl.pallas_call(
        kernel,
        out_shape=out_shape,
        in_specs=[anywhere, smem, vmem] + [anywhere] * 5,
        out_specs=(anywhere,) * 5,
        scratch_shapes=[pltpu.VMEM(*each) for each in scratch]
        + [pltpu.SemaphoreType.DMA((n,)) for n in (DEPARTURES, ARRIVALS, 16)],
        compiler_params=pltpu.CompilerParams(
            collective_id=0, has_side_effects=True, vmem_limit_bytes=56 * 1024 * 1024
        ),
    )(spans, frame_span, norm_gain, w_query, w_key, w_value, w_out, grad_out)
    return pl.pallas_call(
        hand_over,
        out_shape=out_shape,
        in_specs=[vmem] * 5,
        out_specs=(vmem,) * 5,
    )(*results)


def solution(mesh):
    placed = (
        P("dp", "tm", None, "mp"),
        P("dp", "tm"),
        P("mp"),
        P(("dp", "tm"), "mp"),
        P(("dp", "tm"), "mp"),
        P(("dp", "tm"), "mp"),
        P("mp", ("dp", "tm")),
        P("dp", "tm", None, "mp"),
    )
    return jax.shard_map(
        local,
        mesh=mesh,
        in_specs=placed,
        out_specs=(
            P("dp", "tm", None, "mp"),
            P(("dp", "tm"), "mp"),
            P(("dp", "tm"), "mp"),
            P(("dp", "tm"), "mp"),
            P("mp", ("dp", "tm")),
        ),
        check_vma=False,
    )
```

```python
import math

import jax
import jax.numpy as jnp
from jax import lax
from jax.experimental import pallas as pl
from jax.experimental.pallas import tpu as pltpu
from jax.sharding import PartitionSpec as P

HS = 128
EPSILON = 1e-05
BF = jnp.bfloat16
F32 = jnp.float32
MESH = pl.DeviceIdType.MESH
ARRIVALS = 104
DEPARTURES = 4
RULER = 6144

ROWS_COLS = (((1,), (1,)), ((), ()))


def dot(left, right):
    return jnp.dot(left, right, preferred_element_type=F32)


def dot_t(left, right):
    return lax.dot_general(left, right, ROWS_COLS, preferred_element_type=F32)


class Batch:
    def __init__(self, copies, at):
        self.copies = copies
        self.at = at
        self.kib = 0

    def __call__(self, src, dst, device):
        copies = self.copies
        kib = math.prod(dst.shape) * jnp.dtype(dst.dtype).itemsize // 1024
        if copies.departed[-1] + kib > RULER:
            copies.departed.append(0)
        copies.departed[-1] += kib
        self.kib += kib
        pltpu.make_async_remote_copy(
            src_ref=src,
            dst_ref=dst,
            send_sem=copies.send.at[len(copies.departed) - 1],
            recv_sem=copies.recv.at[self.at],
            device_id=device,
            device_id_type=MESH,
        ).start()

    def wait(self):
        copies = self.copies
        copies.open.remove(self)
        copies.wait(copies.recv.at[self.at], self.kib)


class Copies:
    def __init__(self, send, recv, ruler):
        self.send = send
        self.recv = recv
        self.ruler = ruler
        self.departed = [0]
        self.count = 0
        self.open = []

    def batch(self):
        assert self.count < ARRIVALS
        new = Batch(self, self.count)
        self.count += 1
        self.open.append(new)
        return new

    def __call__(self, src, dst, device):
        new = self.batch()
        new(src, dst, device)
        return new

    def wait(self, sem, kib):
        span = self.ruler.at[pl.ds(0, kib)]
        pltpu.make_async_copy(span, span, sem).wait()

    def finish(self):
        assert not self.open
        assert len(self.departed) <= DEPARTURES
        for at, kib in enumerate(self.departed):
            self.wait(self.send.at[at], kib)


def kernel(
    spans_ref,
    which_ref,
    gain_ref,
    wq_ref,
    wk_ref,
    wv_ref,
    wo_ref,
    dy_ref,
    span_out,
    q_out,
    k_out,
    v_out,
    o_out,
    sp,
    xs_in,
    xn,
    dy,
    wl,
    wol,
    wp,
    wg,
    ss,
    sl,
    iv,
    aq,
    aa,
    sb,
    rb,
    so,
    st,
    ob,
    gb,
    gc,
    gt,
    ts,
    tr,
    tl,
    tt,
    ps,
    sr,
    cs,
    cr,
    wt,
    wt_o,
    ra_o,
    ta_o,
    r1_o,
    rc_o,
    tc_o,
    ra,
    ta,
    r1,
    rc,
    tc,
    re,
    re_o,
    oc,
    oc_o,
    span_v,
    g_v,
    o_v,
    ruler,
    send,
    recv,
    near_sem,
):
    dp = lax.axis_index("dp")
    tm = lax.axis_index("tm")
    mp = lax.axis_index("mp")
    core = lax.rem(dp, 2)
    other = 1 - core
    yh = lax.div(dp, 2)
    x = lax.div(tm, 2)
    yl = lax.rem(tm, 2)
    y = yh * 2 + yl

    def hi(v):
        return lax.div(v, 2)

    def lo(v):
        return lax.rem(v, 2)

    def device(x_at, y_at):
        return (hi(y_at) * 2 + core, x_at * 2 + lo(y_at), mp)

    def device_of(x_at, y_at, core_at):
        return (hi(y_at) * 2 + core_at, x_at * 2 + lo(y_at), mp)

    def ring8(offset):
        return lax.rem(mp + offset + 8, 8)

    def along_z(offset):
        return (dp, tm, ring8(offset))

    def along_tm(offset):
        return (dp, lax.rem(tm + offset, 8), mp)

    sibling = (yh * 2 + other, tm, mp)
    zr, zl = along_z(1), along_z(-1)
    xs = tuple(lax.rem(x + k, 4) for k in range(4))
    ys = tuple(lax.rem(y + k, 4) for k in range(4))
    xh = hi(x)
    xr, xl = device(xs[1], y), device(xs[3], y)
    yr, yd = device(x, ys[1]), device(x, ys[3])
    far_y = device(x, lax.rem(y + 3 + 2 * yl, 4))

    barrier = pltpu.get_barrier_semaphore()
    partners = [sibling, far_y]
    partners += [along_z(k) for k in range(1, 8)]
    partners += [along_tm(k) for k in range(1, 8)]
    partners += [device_of(xs[k], y, other) for k in (1, 3)]
    partners += [device_of(x, ys[k], other) for k in (1, 3)]
    for partner in partners:
        pl.semaphore_signal(barrier, inc=1, device_id=partner, device_id_type=MESH)

    fetched = []

    def fetch(src, dst):
        c = pltpu.make_async_copy(src, dst, near_sem.at[len(fetched)])
        c.start()
        fetched.append(c)
        return c

    span_in = fetch(spans_ref.at[0], sp)
    w_in = [fetch(ref, wl.at[a]) for a, ref in enumerate((wq_ref, wk_ref, wv_ref))]
    w_in.append(fetch(wo_ref, wol))
    dy_in = fetch(dy_ref.at[0, 0], dy.at[mp, core])

    which = which_ref[0, 0]
    gain = gain_ref[...].astype(F32).reshape(1, 512)
    span_in.wait()
    xs_in[...] = jnp.where(which == 0, sp[0], sp[1])
    sums = jnp.zeros((256, HS), F32)
    for g in range(4):
        part = xs_in[:, g * HS : (g + 1) * HS].astype(F32)
        sums = sums + part * part
    row = jnp.sum(sums.T, axis=0, keepdims=True)
    sl[...] = jnp.broadcast_to(row, (8, 256))
    for c in w_in:
        c.wait()
    for h in range(2):
        for a in range(3):
            wp[h, :, a * HS : (a + 1) * HS] = wl[a, :, h * HS : (h + 1) * HS]
        wp[h, :, 3 * HS :] = wol[h * HS : (h + 1) * HS, :].astype(F32).T.astype(BF)
    pl.semaphore_wait(barrier, len(partners))

    copy = Copies(send, recv, ruler)

    halves = (
        ((1, 0, 128), (1, 128, 128), (2, 0, 128), (2, 128, 128), (3, 0, 128), (3, 128, 128), (4, 0, 128)),
        ((1, 128, 128), (1, 0, 128), (2, 128, 128), (2, 0, 128), (3, 128, 128), (3, 0, 128), (4, 128, 128)),
    )
    first_half = ((1, 0, 128), (1, 128, 128), (2, 0, 128), (3, 0, 128))
    staged = (
        first_half
        + ((4, 0, 64), (2, 128, 64), (2, 192, 64))
        + ((3, 128, 64), (3, 192, 64), (4, 128, 64)),
        first_half
        + ((4, 64, 64), (2, 192, 64), (2, 128, 64))
        + ((3, 192, 64), (3, 128, 64), (4, 192, 64)),
    )

    class Ring:
        def __init__(self, ref, ways, src):
            self.ref = ref
            self.ways = ways
            self.src = src
            self.flight = {}
            self.pending = {}

        def part(self, d, k, first, rows):
            offset = -k if d == 0 else k
            return self.ref.at[ring8(offset), core, pl.ds(first, rows)]

        def pass_on(self, d, j):
            k, first, rows = self.ways[d][j]
            part = self.part(d, k - 1, first, rows)
            src = self.src.at[pl.ds(first, rows)] if k == 1 else part
            if d == 0:
                self.flight[j] = copy.batch()
            self.flight[j](src, part, (zr, zl)[d])

        def send(self, *which_parts):
            for j in which_parts:
                for d in range(2):
                    self.pass_on(d, j)

        def take(self, *which_parts, then=()):
            for at, j in enumerate(which_parts):
                self.flight[j].wait()
                if then:
                    self.send(then[at])

        def share(self, *which_parts, half=0):
            for d in range(2):
                rows = [self.ways[d][j] for j in which_parts]
                first = min(r[1] for r in rows)
                part = self.part(d, rows[0][0], first, sum(r[2] for r in rows))
                self.hand(part, half)

        def hand(self, part, half=0):
            if half not in self.pending:
                self.pending[half] = copy.batch()
            self.pending[half](part, part, sibling)

        def settle(self, half=0):
            if half in self.pending:
                self.pending.pop(half).wait()

    grad_in = dy_ref.at[0, 0]
    ring_dy = Ring(dy, staged, grad_in)
    sumsq = copy.batch()
    for k in range(1, 8):
        sumsq(sl, ss.at[mp], along_z(k))
    ss[mp] = sl[...]
    mine = wg.at[yh, core, xh, lo(x), yl]
    pair = copy(wp.at[other], mine, sibling)
    ring_dy.send(0, 1)
    wg[yh, core, xh, lo(x), yl] = wp[core]

    class Spread:
        def __init__(self, at, ring, right, left):
            self.at = at
            self.ring = ring
            self.to = (right, left)
            own = at(ring[0])
            self.trip = copy.batch()
            self.trip(own, own, right)
            self.trip(own, own, left)

        def relay(self):
            self.trip.wait()
            self.trip = copy.batch()
            part = self.at(self.ring[3]).at[pl.ds(0, 64)]
            self.trip(part, part, self.to[0])
            part = self.at(self.ring[1]).at[pl.ds(64, 64)]
            self.trip(part, part, self.to[1])

        def done(self):
            self.trip.wait()

    def block(x_at, y_at, s):
        return wg.at[hi(y_at), s, hi(x_at), lo(x_at), lo(y_at)]

    def spread_a(k):
        return Spread(lambda v: block(xs[k], v, 0), ys, yr, yd)

    def spread_b(k):
        return Spread(lambda v: block(v, ys[k], 1), xs, xr, xl)

    pair.wait()
    a1 = Spread(lambda v: block(v, y, 0), xs, xr, xl)
    b1 = Spread(lambda v: block(x, v, 1), ys, yr, yd)
    second = {0: (spread_a(0), spread_b(0))}

    sumsq.wait()
    total = ss[0]
    for k in range(1, 8):
        total = total + ss[k]
    inv_row = lax.rsqrt(total / 4096.0 + EPSILON)
    iv[...] = jnp.broadcast_to(inv_row[0:1, :], (HS, 256)).T
    for g in range(4):
        cols = slice(g * HS, (g + 1) * HS)
        xn[mp, core, :, cols] = (
            xs_in[:, cols].astype(F32) * iv[...] * gain[:, cols]
        ).astype(BF)
    ring_xn = Ring(xn, halves, xn.at[mp, core])
    ring_xn.send(0, 1)
    ring_xn.hand(xn.at[mp, core])
    ring_dy.take(0, then=(2,))
    aq[...] = jnp.zeros_like(aq)
    aa[...] = jnp.zeros_like(aa)

    a1.relay()
    b1.relay()
    for k in (3, 1):
        second[k] = (spread_a(k), spread_b(k))

    def relay(k):
        second[k][0].relay()
        second[k][1].relay()

    relay(0)
    dy_in.wait()
    ring_dy.hand(dy.at[mp, core, pl.ds(0, 128)], 0)
    ring_dy.hand(dy.at[mp, core, pl.ds(128, 128)], 1)
    ring_dy.take(1)
    ring_dy.share(0)
    ring_dy.share(1, half=1)
    a1.done()
    b1.done()
    second[2] = (spread_a(2), spread_b(2))
    ring_xn.take(0, then=(2,))
    ring_xn.take(1, then=(3,))
    ring_xn.share(0, 1)
    relay(3)
    ring_dy.take(2, then=(3,))
    ring_dy.share(2)
    relay(1)
    ring_xn.take(2, then=(4,))
    relay(2)
    ring_xn.take(3, then=(5,))
    ring_xn.share(2, 3)
    ring_dy.take(3, then=(4,))
    ring_dy.share(3)
    for k in range(4):
        second[k][0].done()
        second[k][1].done()

    def weights(m, cols):
        return wg[lax.div(m, 4), lo(hi(m)), lo(m), :, :, :, cols].reshape(512, -1)

    qkv_cols = slice(0, 3 * HS)
    out_cols = slice(3 * HS, 4 * HS)

    def forward(ref, into, cols, rows, first, step, count):
        def body(i, carry):
            m = ring8(first + step * i)
            shape = (2, rows.stop - rows.start)
            left = ref[m, :, rows].reshape(shape[0] * shape[1], 512)
            into[:, rows] += dot(left, weights(m, cols)).reshape(*shape, -1)
            return carry

        lax.fori_loop(0, count, body, 0)

    def forward_xn(*which_chunks):
        ring_xn.settle()
        forward(xn, aq, qkv_cols, slice(0, 256), *which_chunks)

    def group(half):
        return slice(half * 128, half * 128 + 128)

    def forward_dy(half, *which_chunks):
        ring_dy.settle(half)
        forward(dy, aa, out_cols, group(half), *which_chunks)

    forward_xn(-1, 1, 3)
    ring_xn.take(4, then=(6,))
    ring_dy.send(5, 6)
    forward_dy(0, -1, 1, 3)
    ring_xn.take(5)
    ring_xn.share(4, 5)
    forward_xn(-2, 4, 2)
    ring_dy.take(4)
    ring_dy.hand(dy.at[ring8(4), core, pl.ds(0, 128)])
    forward_dy(0, -2, 4, 2)
    forward_dy(0, -3, 6, 2)
    forward_xn(-3, 6, 2)
    ring_xn.take(6)
    ring_xn.hand(xn.at[ring8(4), core])
    forward_dy(0, 4, 0, 1)

    def strip(at):
        return pl.ds(pl.multiple_of(at * 16, 16), 16)

    def swap_out(arrays, parts):
        trips = copy.batch()
        for k in range(1, 8):
            src = sb.at[arrays, parts, :, strip(lax.rem(tm + k, 8))]
            trips(src, rb.at[arrays, parts, :, tm], along_tm(k))
        rb[arrays, parts, :, tm] = sb[arrays, parts, :, strip(tm), :]
        return trips

    def swap_back(arrays, parts):
        trips = copy.batch()
        for k in range(1, 8):
            dst = gb.at[arrays, parts, :, strip(tm)]
            trips(ob.at[arrays, parts, :, lax.rem(tm + k, 8)], dst, along_tm(k))
        gb[arrays, parts, :, strip(tm), :] = ob[arrays, parts, :, tm]
        return trips

    both = pl.ds(0, 2)
    one = (pl.ds(0, 1), pl.ds(1, 1))

    def grads_out(part):
        for s in range(2):
            sb[3, part, s] = aa[s, group(part)].astype(BF)
        return swap_out(pl.ds(3, 1), one[part])

    away = [grads_out(0)]
    forward_xn(4, 0, 1)
    for s in range(2):
        for a in range(3):
            for part in range(2):
                sb[a, part, s] = aq[s, group(part), a * HS : (a + 1) * HS].astype(BF)
    trips = swap_out(pl.ds(0, 3), both)
    ring_dy.take(5, then=(7,))
    ring_dy.take(6, then=(8,))
    ring_dy.share(5, 6, half=1)
    forward_dy(1, -1, 1, 3)
    ring_dy.take(7, then=(9,))
    forward_dy(1, -2, 4, 2)
    ring_dy.take(8)
    ring_dy.share(7, 8, half=1)
    forward_dy(1, -3, 6, 2)
    ring_dy.take(9)
    ring_dy.hand(dy.at[ring8(4), core, pl.ds(128, 128)], 1)
    trips.wait()

    row_id = lax.broadcasted_iota(jnp.int32, (256, 256), 0)
    col_id = lax.broadcasted_iota(jnp.int32, (256, 256), 1)
    same = ((row_id & 15) == (col_id & 15)) & ((row_id >> 7) == (col_id >> 7))
    seen = same & ((row_id >> 4) >= (col_id >> 4))
    scale = HS ** (-0.5)

    def held(i, part):
        return rb[i, part].reshape(256, HS)

    def attend(part):
        q, k, v = (held(i, part) for i in range(3))
        scores = jnp.where(seen, dot_t(q, k) * scale, -1e30)
        expo = jnp.exp(scores - jnp.max(scores, axis=1, keepdims=True))
        soft = expo / jnp.sum(expo, axis=1, keepdims=True)
        so[part] = soft
        st[part] = soft.T.astype(BF)
        ob[0, part] = dot(soft.astype(BF), v).astype(BF).reshape(2, 8, 16, HS)

    def attend_back(part):
        away[part].wait()
        q, k, v, a = (held(i, part) for i in range(4))
        soft = so[part]
        dsoft = dot_t(a, v)
        dscore = soft * (dsoft - jnp.sum(dsoft * soft, axis=1, keepdims=True)) * scale
        results = (
            dot(dscore.astype(BF), k),
            dot(dscore.T.astype(BF), q),
            dot(st[part], a),
        )
        for i, value in enumerate(results):
            ob[1 + i, part] = value.astype(BF).reshape(2, 8, 16, HS)
        return swap_back(pl.ds(1, 3), one[part])

    attend(0)
    forward_dy(1, 4, 0, 1)
    away.append(grads_out(1))
    back = [attend_back(0)]
    attend(1)
    att_trips = swap_back(pl.ds(0, 1), both)
    back.append(attend_back(1))

    def keep_transposed(a):
        for part in range(2):
            for s in range(2):
                first = s * 256 + part * 128
                source = gb[(a + 1) % 4, part, s].astype(F32)
                gt[a * HS : (a + 1) * HS, first : first + 128] = source.T.astype(BF)

    def out_grad(m, carry):
        value = dot(gt[3 * HS :, :], dy[m].reshape(512, 512)).astype(BF)
        place = wt_o.at[lax.div(m, 4), lo(hi(m)), lo(m)]
        for i in range(4):
            place[i // 2, i % 2] = value[:, i * HS : (i + 1) * HS]
        return carry


    offsets = (4, 3, -3, 2, -2, 1, -1, 0)

    def grads_in(half):
        for s in range(2):
            for a in range(3):
                gc[s, group(half), a * HS : (a + 1) * HS] = gb[1 + a, half, s]

    needs = (((0, 2), (1, 4), (3, 6), (5, 7)), ((0, 1), (3, 2), (5, 4), (6, 7)))

    def input_grads(half, order):
        met = copy.batch()
        rows = group(half)
        for index in needs[half][order]:
            w = weights(ring8(offsets[index]), qkv_cols)
            value = dot_t(gc[:, rows, :].reshape(256, 3 * HS), w).astype(BF)
            ps[index, :, rows, :] = value.reshape(2, 128, 512)
            part = pl.ds(half * 128, 128)
            met(ps.at[index, other, part], sr.at[index, part], sibling)
        across[half, order] = met

    across = {}

    def total_of(index, rows):
        return ps[index, core, rows, :].astype(F32) + sr[index, rows, :].astype(F32)

    ways = (((4, 3, 2, 1), (3, 2, 1)), ((3, 2, 1), (4, 3, 2, 1)))
    flying = {}

    def hop(half, order):
        across.pop((half, order)).wait()
        slot = half * 4 + order
        for quarter in range(2):
            if order:
                flying[half, quarter].wait()
            trip = copy.batch()
            flying[half, quarter] = trip
            part = slice(quarter * 64, quarter * 64 + 64)
            rows = slice(half * 128 + part.start, half * 128 + part.stop)
            for d in range(2):
                way = ways[half][d]
                if order >= len(way):
                    continue
                distance = way[order]
                offset = 4 if distance == 4 else (distance, -distance)[d]
                value = total_of(offsets.index(offset), rows)
                if order:
                    value = value + cr[d, slot - 1, part, :].astype(F32)
                cs[d, slot, part, :] = value.astype(BF)
                place = (d, slot, pl.ds(part.start, 64))
                trip(cs.at[place], cr.at[place], (zr, zl)[d])

    class Reduce:
        def __init__(self, part, right, left, got, tmp, end=None):
            self.part = part
            self.to = (right, left)
            self.got = got
            self.tmp = tmp
            self.ends, self.slots, self.second = end or (self.to, got, None)

        def far(self):
            self.first = copy.batch()
            self.first(self.part(2, 0), self.got.at[0], self.to[0])
            self.first(self.part(2, 1), self.got.at[1], self.to[1])

        def near(self):
            if self.second is None:
                self.second = copy.batch()
            self.second(self.part(1, 1), self.slots.at[2], self.ends[0])
            self.second(self.part(3, 0), self.slots.at[3], self.ends[1])

        def chain(self):
            self.first.wait()
            for d, (at, half) in enumerate(((1, 0), (3, 1))):
                value = self.part(at, half)[...].astype(F32) + self.got[d].astype(F32)
                self.tmp[d] = value.astype(BF)
                self.second(self.tmp.at[d], self.slots.at[4 + d], self.ends[d])

        def finish(self):
            self.second.wait()
            return joined(self.part(0, 0)[...], self.part(0, 1)[...], self.slots)

    def joined(first, second, got):
        return (
            first.astype(F32) + got[3].astype(F32) + got[4].astype(F32),
            second.astype(F32) + got[2].astype(F32) + got[5].astype(F32),
        )

    ending = copy.batch()

    def end_of(axis, slots):
        if axis == 0:
            ends = device_of(xs[1], y, axis), device_of(xs[3], y, axis)
        else:
            ends = device_of(x, ys[1], axis), device_of(x, ys[3], axis)
        return ends, slots.at[core], ending

    def out_first(axis):
        def part_a(j, half):
            return wt_o.at[hi(ys[j]), 0, half, :, lo(ys[j])]

        def part_b(j, half):
            return wt_o.at[half, 1, hi(xs[j]), lo(xs[j]), :]

        part, right, left = ((part_a, yr, yd), (part_b, xr, xl))[axis]
        return Reduce(part, right, left, ra_o.at[axis], ta_o.at[axis])

    def out_second(axis):
        ring = (xs, ys)[axis]

        def part(j, half):
            return r1_o.at[axis, hi(ring[j]), lo(ring[j]), pl.ds(half * 64, 64)]

        right, left = ((xr, xl), (yr, yd))[axis]
        end = end_of(axis, re_o)
        return Reduce(part, right, left, rc_o.at[axis], tc_o.at[axis], end)

    out1 = [out_first(axis) for axis in range(2)]
    out2 = [out_second(axis) for axis in range(2)]
    back[0].wait()
    grads_in(0)
    input_grads(0, 0)
    att_trips.wait()
    keep_transposed(3)
    lax.fori_loop(0, 8, out_grad, 0)
    for stage in out1:
        stage.far()
        stage.near()
    hop(0, 0)
    input_grads(0, 1)
    back[1].wait()
    grads_in(1)
    input_grads(1, 0)

    for a in range(3):
        keep_transposed(a)

    def weight_grad(yh_at, s_at, xh_at):
        m = (yh_at * 2 + s_at) * 2 + xh_at
        value = dot(gt[: 3 * HS, :], xn[m].reshape(512, 512)).astype(BF)
        for i in range(4):
            wt[yh_at, s_at, xh_at, i // 2, i % 2] = value[:, i * HS : (i + 1) * HS]

    def grads(which_chunk):
        def body(i, carry):
            weight_grad(*which_chunk(i))
            return carry

        lax.fori_loop(0, 2, body, 0)

    def half_rows(half):
        return slice(half * 192, half * 192 + 192)

    def first_stage(axis, k):
        def part_a(j, half):
            at = ys[j]
            return wt.at[hi(at), 0, hi(xs[k]), lo(xs[k]), lo(at), half_rows(half)]

        def part_b(j, half):
            at = xs[j]
            return wt.at[hi(ys[k]), 1, hi(at), lo(at), lo(ys[k]), half_rows(half)]

        part, right, left = ((part_a, yr, yd), (part_b, xr, xl))[axis]
        return Reduce(part, right, left, ra.at[axis, k], ta.at[axis, k])

    def second_stage(axis):
        def part(j, half):
            return r1.at[axis, j, half_rows(half)]

        right, left = ((xr, xl), (yr, yd))[axis]
        end = end_of(axis, re)
        return Reduce(part, right, left, rc.at[axis], tc.at[axis], end)

    stage1 = [[first_stage(axis, k) for k in range(4)] for axis in range(2)]
    stage2 = [second_stage(axis) for axis in range(2)]

    def chain(k):
        for axis in range(2):
            stage1[axis][k].chain()

    def finish(k):
        for axis in range(2):
            for half, value in enumerate(stage1[axis][k].finish()):
                r1[axis, k, half_rows(half), :] = value.astype(BF)

    def start(axis, *groups):
        for k in groups:
            stage1[axis][k].far()
            stage1[axis][k].near()

    grads(lambda i: (i, 0, 1 - xh))
    start(0, 2)
    hop(1, 0)
    grads(lambda i: (1 - yh, 1, i))
    start(1, 2)
    grads(lambda i: (i, 0, xh))
    start(0, 1, 3, 0)
    hop(0, 1)
    grads(lambda i: (yh, 1, i))
    start(1, 1, 3, 0)
    input_grads(1, 1)
    chain(2)
    for stage in out1:
        stage.chain()
    input_grads(0, 2)
    hop(1, 1)
    hop(0, 2)
    input_grads(1, 2)

    for s in range(2):
        prod = jnp.zeros((256, HS), F32)
        for a in range(3):
            left = jnp.concatenate([gb[1 + a, part, s] for part in range(2)], axis=0)
            right = jnp.concatenate([sb[a, part, s] for part in range(2)], axis=0)
            prod = prod + left.astype(F32) * right.astype(F32)
        ts[s] = jnp.broadcast_to(jnp.sum(prod.T, axis=0, keepdims=True), (8, 256))
    inner_pair = copy(ts.at[other], tr, sibling)

    chain(1)
    chain(3)
    finish(2)
    for axis in range(2):
        stage2[axis].far()
    hop(1, 2)
    input_grads(0, 3)
    input_grads(1, 3)
    chain(0)
    hop(0, 3)
    for axis in range(2):
        for half, value in enumerate(out1[axis].finish()):
            r1_o[axis, half] = value.astype(BF)
        out2[axis].far()
        out2[axis].near()
    inner_pair.wait()
    tl[...] = ts[core] + tr[...]
    tt[mp] = tl[...]
    inner = copy.batch()
    for k in range(1, 8):
        inner(tl, tt.at[mp], along_z(k))
    finish(1)
    finish(3)
    for axis in range(2):
        stage2[axis].near()
    hop(1, 3)
    for stage in out2:
        stage.chain()
    finish(0)
    for axis in range(2):
        stage2[axis].chain()

    def out_place(axis):
        return r1_o.at[axis, xh + axis * (yh - xh), lo(x) + axis * (yl - lo(x))]

    ending(r1.at[other, 0], oc.at[core], sibling)
    ending(out_place(other), oc_o.at[core], sibling)
    oc[core] = r1[core, 0]
    oc_o[core] = out_place(core)[...]

    inner.wait()
    inner_row = tt[0]
    for k in range(1, 8):
        inner_row = inner_row + tt[k]
    inner_col = jnp.broadcast_to(inner_row[0:1, :] / 4096.0, (HS, 256)).T
    for half in range(2):
        rows = group(half)
        for quarter in range(2):
            flying[half, quarter].wait()
        grad = total_of(7, rows)
        for d in range(2):
            final = len(ways[half][d]) - 1
            grad = grad + cr[d, half * 4 + final].astype(F32)
        inverse = iv[rows, :]
        back = inverse * inverse * inner_col[rows, :]
        for g in range(4):
            cols = slice(g * HS, (g + 1) * HS)
            scaled = grad[:, cols] * gain[:, cols]
            branch = inverse * scaled - xs_in[rows, cols].astype(F32) * back
            value = (dy[mp, core, rows, cols].astype(F32) + branch).astype(BF)
            for j in range(2):
                span_v[j, rows, cols] = jnp.where(which == j, value, jnp.zeros_like(value))
    written = [fetch(span_v, span_out.at[0])]

    ending.wait()
    for h in range(2):
        cols = slice(h * HS, (h + 1) * HS)
        halves_of = joined(oc[h, :192, :], oc[h, 192:, :], re.at[h])
        whole = jnp.concatenate(halves_of, axis=0)
        for a in range(3):
            g_v[a, :, cols] = whole[a * HS : (a + 1) * HS, :].T
        first, second = joined(oc_o[h, :64, :], oc_o[h, 64:, :], re_o.at[h])
        o_v[h * HS : h * HS + 64, :] = first
        o_v[h * HS + 64 : (h + 1) * HS, :] = second
    for a, ref in enumerate((q_out, k_out, v_out)):
        written.append(fetch(g_v.at[a], ref))
    written.append(fetch(o_v, o_out))
    copy.finish()
    for c in written:
        c.wait()


def hand_over(*refs):
    ins, outs, held, sems = refs[:5], refs[5:10], refs[10:15], refs[15]
    fetched = [pltpu.make_async_copy(ins[i], held[i], sems.at[0, i]) for i in range(5)]
    written = [pltpu.make_async_copy(held[i], outs[i], sems.at[1, i]) for i in range(5)]
    for c in fetched:
        c.start()
    for i in range(5):
        fetched[i].wait()
        written[i].start()
    for c in written:
        c.wait()


def local(spans, frame_span, norm_gain, w_query, w_key, w_value, w_out, grad_out):
    vmem = pl.BlockSpec(memory_space=pltpu.VMEM)
    smem = pl.BlockSpec(memory_space=pltpu.SMEM)
    anywhere = pl.BlockSpec(memory_space=pl.ANY)
    shape = jax.ShapeDtypeStruct
    scratch = [
        ((2, 256, 512), BF),
        ((256, 512), BF),
        ((8, 2, 256, 512), BF),
        ((8, 2, 256, 512), BF),
        ((3, 128, 256), BF),
        ((256, 128), BF),
        ((2, 128, 512), BF),
        ((2, 2, 2, 2, 2, 128, 512), BF),
        ((8, 8, 256), F32),
        ((8, 256), F32),
        ((256, 128), F32),
        ((2, 256, 384), F32),
        ((2, 256, 128), F32),
        ((4, 2, 2, 128, 128), BF),
        ((4, 2, 2, 8, 16, 128), BF),
        ((2, 256, 256), F32),
        ((2, 256, 256), BF),
        ((4, 2, 2, 8, 16, 128), BF),
        ((4, 2, 2, 128, 128), BF),
        ((2, 256, 384), BF),
        ((512, 512), BF),
        ((2, 8, 256), F32),
        ((8, 256), F32),
        ((8, 256), F32),
        ((8, 8, 256), F32),
        ((8, 2, 256, 512), BF),
        ((8, 256, 512), BF),
        ((2, 8, 128, 512), BF),
        ((2, 8, 128, 512), BF),
        ((2, 2, 2, 2, 2, 384, 128), BF),
        ((2, 2, 2, 2, 2, 128, 128), BF),
        ((2, 6, 2, 128, 128), BF),
        ((2, 2, 2, 128, 128), BF),
        ((2, 2, 2, 128, 128), BF),
        ((2, 6, 64, 128), BF),
        ((2, 2, 64, 128), BF),
        ((2, 4, 6, 192, 128), BF),
        ((2, 4, 2, 192, 128), BF),
        ((2, 4, 384, 128), BF),
        ((2, 6, 192, 128), BF),
        ((2, 2, 192, 128), BF),
        ((2, 6, 192, 128), BF),
        ((2, 6, 64, 128), BF),
        ((2, 384, 128), BF),
        ((2, 128, 128), BF),
        ((2, 256, 512), BF),
        ((3, 128, 256), F32),
        ((256, 128), F32),
        ((RULER, 256), F32),
    ]
    out_shape = (
        shape((1, 2, 256, 512), BF),
        shape((128, 256), F32),
        shape((128, 256), F32),
        shape((128, 256), F32),
        shape((256, 128), F32),
    )
    results = pl.pallas_call(
        kernel,
        out_shape=out_shape,
        in_specs=[anywhere, smem, vmem] + [anywhere] * 5,
        out_specs=(anywhere,) * 5,
        scratch_shapes=[pltpu.VMEM(*each) for each in scratch]
        + [pltpu.SemaphoreType.DMA((n,)) for n in (DEPARTURES, ARRIVALS, 11)],
        compiler_params=pltpu.CompilerParams(
            collective_id=0, has_side_effects=True, vmem_limit_bytes=56 * 1024 * 1024
        ),
    )(spans, frame_span, norm_gain, w_query, w_key, w_value, w_out, grad_out)
    return pl.pallas_call(
        hand_over,
        out_shape=out_shape,
        in_specs=[anywhere] * 5,
        out_specs=(anywhere,) * 5,
        scratch_shapes=[pltpu.VMEM(each.shape, each.dtype) for each in out_shape]
        + [pltpu.SemaphoreType.DMA((2, 5))],
    )(*results)


def solution(mesh):
    placed = (
        P("dp", "tm", None, "mp"),
        P("dp", "tm"),
        P("mp"),
        P(("dp", "tm"), "mp"),
        P(("dp", "tm"), "mp"),
        P(("dp", "tm"), "mp"),
        P("mp", ("dp", "tm")),
        P("dp", "tm", None, "mp"),
    )
    return jax.shard_map(
        local,
        mesh=mesh,
        in_specs=placed,
        out_specs=(
            P("dp", "tm", None, "mp"),
            P(("dp", "tm"), "mp"),
            P(("dp", "tm"), "mp"),
            P(("dp", "tm"), "mp"),
            P("mp", ("dp", "tm")),
        ),
        check_vma=False,
    )
```

```python
import math

import jax
import jax.numpy as jnp
from jax import lax
from jax.experimental import pallas as pl
from jax.experimental.pallas import tpu as pltpu
from jax.sharding import PartitionSpec as P

HS = 128
EPSILON = 1e-05
BF = jnp.bfloat16
F32 = jnp.float32
MESH = pl.DeviceIdType.MESH
ARRIVALS = 104
DEPARTURES = 4
RULER = 6144

ROWS_COLS = (((1,), (1,)), ((), ()))


def dot(left, right):
    return jnp.dot(left, right, preferred_element_type=F32)


def dot_t(left, right):
    return lax.dot_general(left, right, ROWS_COLS, preferred_element_type=F32)


class Batch:
    def __init__(self, copies, at):
        self.copies = copies
        self.at = at
        self.kib = 0

    def __call__(self, src, dst, device):
        copies = self.copies
        kib = math.prod(dst.shape) * jnp.dtype(dst.dtype).itemsize // 1024
        if copies.departed[-1] + kib > RULER:
            copies.departed.append(0)
        copies.departed[-1] += kib
        self.kib += kib
        pltpu.make_async_remote_copy(
            src_ref=src,
            dst_ref=dst,
            send_sem=copies.send.at[len(copies.departed) - 1],
            recv_sem=copies.recv.at[self.at],
            device_id=device,
            device_id_type=MESH,
        ).start()

    def wait(self):
        copies = self.copies
        copies.open.remove(self)
        copies.wait(copies.recv.at[self.at], self.kib)


class Copies:
    def __init__(self, send, recv, ruler):
        self.send = send
        self.recv = recv
        self.ruler = ruler
        self.departed = [0]
        self.count = 0
        self.open = []

    def batch(self):
        assert self.count < ARRIVALS
        new = Batch(self, self.count)
        self.count += 1
        self.open.append(new)
        return new

    def __call__(self, src, dst, device):
        new = self.batch()
        new(src, dst, device)
        return new

    def wait(self, sem, kib):
        span = self.ruler.at[pl.ds(0, kib)]
        pltpu.make_async_copy(span, span, sem).wait()

    def finish(self):
        assert not self.open
        assert len(self.departed) <= DEPARTURES
        for at, kib in enumerate(self.departed):
            self.wait(self.send.at[at], kib)


def kernel(
    spans_ref,
    which_ref,
    gain_ref,
    wq_ref,
    wk_ref,
    wv_ref,
    wo_ref,
    dy_ref,
    span_out,
    q_out,
    k_out,
    v_out,
    o_out,
    sp,
    xs_in,
    xn,
    dy,
    wl,
    wol,
    wp,
    wg,
    ss,
    sl,
    iv,
    aq,
    aa,
    sb,
    rb,
    so,
    st,
    ob,
    gb,
    gc,
    gt,
    ts,
    tr,
    tl,
    tt,
    ps,
    sr,
    cs,
    cr,
    wt,
    wt_o,
    ra_o,
    ta_o,
    r1_o,
    rc_o,
    tc_o,
    ra,
    ta,
    r1,
    rc,
    tc,
    re,
    re_o,
    oc,
    oc_o,
    span_v,
    g_v,
    o_v,
    ruler,
    send,
    recv,
    near_sem,
):
    dp = lax.axis_index("dp")
    tm = lax.axis_index("tm")
    mp = lax.axis_index("mp")
    core = lax.rem(dp, 2)
    other = 1 - core
    yh = lax.div(dp, 2)
    x = lax.div(tm, 2)
    yl = lax.rem(tm, 2)
    y = yh * 2 + yl

    def hi(v):
        return lax.div(v, 2)

    def lo(v):
        return lax.rem(v, 2)

    def device(x_at, y_at):
        return (hi(y_at) * 2 + core, x_at * 2 + lo(y_at), mp)

    def device_of(x_at, y_at, core_at):
        return (hi(y_at) * 2 + core_at, x_at * 2 + lo(y_at), mp)

    def ring8(offset):
        return lax.rem(mp + offset + 8, 8)

    def along_z(offset):
        return (dp, tm, ring8(offset))

    def along_tm(offset):
        return (dp, lax.rem(tm + offset, 8), mp)

    sibling = (yh * 2 + other, tm, mp)
    zr, zl = along_z(1), along_z(-1)
    xs = tuple(lax.rem(x + k, 4) for k in range(4))
    ys = tuple(lax.rem(y + k, 4) for k in range(4))
    xh = hi(x)
    xr, xl = device(xs[1], y), device(xs[3], y)
    yr, yd = device(x, ys[1]), device(x, ys[3])
    far_y = device(x, lax.rem(y + 3 + 2 * yl, 4))

    barrier = pltpu.get_barrier_semaphore()
    partners = [sibling, far_y]
    partners += [along_z(k) for k in range(1, 8)]
    partners += [along_tm(k) for k in range(1, 8)]
    partners += [device_of(xs[k], y, other) for k in (1, 3)]
    partners += [device_of(x, ys[k], other) for k in (1, 3)]
    for partner in partners:
        pl.semaphore_signal(barrier, inc=1, device_id=partner, device_id_type=MESH)

    fetched = []

    def fetch(src, dst):
        c = pltpu.make_async_copy(src, dst, near_sem.at[len(fetched)])
        c.start()
        fetched.append(c)
        return c

    span_in = fetch(spans_ref.at[0], sp)
    w_in = [fetch(ref, wl.at[a]) for a, ref in enumerate((wq_ref, wk_ref, wv_ref))]
    w_in.append(fetch(wo_ref, wol))
    dy_in = fetch(dy_ref.at[0, 0], dy.at[mp, core])

    which = which_ref[0, 0]
    gain = gain_ref[...].astype(F32).reshape(1, 512)
    span_in.wait()
    xs_in[...] = jnp.where(which == 0, sp[0], sp[1])
    sums = jnp.zeros((256, HS), F32)
    for g in range(4):
        part = xs_in[:, g * HS : (g + 1) * HS].astype(F32)
        sums = sums + part * part
    row = jnp.sum(sums.T, axis=0, keepdims=True)
    sl[...] = jnp.broadcast_to(row, (8, 256))
    for c in w_in:
        c.wait()
    for h in range(2):
        for a in range(3):
            wp[h, :, a * HS : (a + 1) * HS] = wl[a, :, h * HS : (h + 1) * HS]
        wp[h, :, 3 * HS :] = wol[h * HS : (h + 1) * HS, :].astype(F32).T.astype(BF)
    pl.semaphore_wait(barrier, len(partners))

    copy = Copies(send, recv, ruler)

    halves = (
        ((1, 0, 128), (1, 128, 128), (2, 0, 128), (2, 128, 128), (3, 0, 128), (3, 128, 128), (4, 0, 128)),
        ((1, 128, 128), (1, 0, 128), (2, 128, 128), (2, 0, 128), (3, 128, 128), (3, 0, 128), (4, 128, 128)),
    )
    first_half = ((1, 0, 128), (1, 128, 128), (2, 0, 128), (3, 0, 128))
    staged = (
        first_half
        + ((4, 0, 64), (2, 128, 64), (2, 192, 64))
        + ((3, 128, 64), (3, 192, 64), (4, 128, 64)),
        first_half
        + ((4, 64, 64), (2, 192, 64), (2, 128, 64))
        + ((3, 192, 64), (3, 128, 64), (4, 192, 64)),
    )

    class Ring:
        def __init__(self, ref, ways, src):
            self.ref = ref
            self.ways = ways
            self.src = src
            self.flight = {}
            self.pending = {}

        def part(self, d, k, first, rows):
            offset = -k if d == 0 else k
            return self.ref.at[ring8(offset), core, pl.ds(first, rows)]

        def pass_on(self, d, j):
            k, first, rows = self.ways[d][j]
            part = self.part(d, k - 1, first, rows)
            src = self.src.at[pl.ds(first, rows)] if k == 1 else part
            if d == 0:
                self.flight[j] = copy.batch()
            self.flight[j](src, part, (zr, zl)[d])

        def send(self, *which_parts):
            for j in which_parts:
                for d in range(2):
                    self.pass_on(d, j)

        def take(self, *which_parts, then=()):
            for at, j in enumerate(which_parts):
                self.flight[j].wait()
                if then:
                    self.send(then[at])

        def share(self, *which_parts, half=0):
            for d in range(2):
                rows = [self.ways[d][j] for j in which_parts]
                first = min(r[1] for r in rows)
                part = self.part(d, rows[0][0], first, sum(r[2] for r in rows))
                self.hand(part, half)

        def hand(self, part, half=0):
            if half not in self.pending:
                self.pending[half] = copy.batch()
            self.pending[half](part, part, sibling)

        def settle(self, half=0):
            if half in self.pending:
                self.pending.pop(half).wait()

    grad_in = dy_ref.at[0, 0]
    ring_dy = Ring(dy, staged, grad_in)
    sumsq = copy.batch()
    for k in range(1, 8):
        sumsq(sl, ss.at[mp], along_z(k))
    ss[mp] = sl[...]
    mine = wg.at[yh, core, xh, lo(x), yl]
    pair = copy(wp.at[other], mine, sibling)
    ring_dy.send(0, 1)
    wg[yh, core, xh, lo(x), yl] = wp[core]

    class Spread:
        def __init__(self, at, ring, right, left):
            self.at = at
            self.ring = ring
            self.to = (right, left)
            own = at(ring[0])
            self.trip = copy.batch()
            self.trip(own, own, right)
            self.trip(own, own, left)

        def relay(self):
            self.trip.wait()
            self.trip = copy.batch()
            part = self.at(self.ring[3]).at[pl.ds(0, 64)]
            self.trip(part, part, self.to[0])
            part = self.at(self.ring[1]).at[pl.ds(64, 64)]
            self.trip(part, part, self.to[1])

        def done(self):
            self.trip.wait()

    def block(x_at, y_at, s):
        return wg.at[hi(y_at), s, hi(x_at), lo(x_at), lo(y_at)]

    def spread_a(k):
        return Spread(lambda v: block(xs[k], v, 0), ys, yr, yd)

    def spread_b(k):
        return Spread(lambda v: block(v, ys[k], 1), xs, xr, xl)

    pair.wait()
    a1 = Spread(lambda v: block(v, y, 0), xs, xr, xl)
    b1 = Spread(lambda v: block(x, v, 1), ys, yr, yd)
    second = {0: (spread_a(0), spread_b(0))}

    sumsq.wait()
    total = ss[0]
    for k in range(1, 8):
        total = total + ss[k]
    inv_row = lax.rsqrt(total / 4096.0 + EPSILON)
    iv[...] = jnp.broadcast_to(inv_row[0:1, :], (HS, 256)).T
    for g in range(4):
        cols = slice(g * HS, (g + 1) * HS)
        xn[mp, core, :, cols] = (
            xs_in[:, cols].astype(F32) * iv[...] * gain[:, cols]
        ).astype(BF)
    ring_xn = Ring(xn, halves, xn.at[mp, core])
    ring_xn.send(0, 1)
    ring_xn.hand(xn.at[mp, core])
    ring_dy.take(0, then=(2,))
    aq[...] = jnp.zeros_like(aq)
    aa[...] = jnp.zeros_like(aa)

    a1.relay()
    b1.relay()
    for k in (3, 1):
        second[k] = (spread_a(k), spread_b(k))

    def relay(k):
        second[k][0].relay()
        second[k][1].relay()

    relay(0)
    dy_in.wait()
    ring_dy.hand(dy.at[mp, core, pl.ds(0, 128)], 0)
    ring_dy.hand(dy.at[mp, core, pl.ds(128, 128)], 1)
    ring_dy.take(1)
    ring_dy.share(0)
    ring_dy.share(1, half=1)
    a1.done()
    b1.done()
    second[2] = (spread_a(2), spread_b(2))
    ring_xn.take(0, then=(2,))
    ring_xn.take(1, then=(3,))
    ring_xn.share(0, 1)
    relay(3)
    ring_dy.take(2, then=(3,))
    ring_dy.share(2)
    relay(1)
    ring_xn.take(2, then=(4,))
    relay(2)
    ring_xn.take(3, then=(5,))
    ring_xn.share(2, 3)
    ring_dy.take(3, then=(4,))
    ring_dy.share(3)
    for k in range(4):
        second[k][0].done()
        second[k][1].done()

    def weights(m, cols):
        return wg[lax.div(m, 4), lo(hi(m)), lo(m), :, :, :, cols].reshape(512, -1)

    qkv_cols = slice(0, 3 * HS)
    out_cols = slice(3 * HS, 4 * HS)

    def forward(ref, into, cols, rows, first, step, count):
        def body(i, carry):
            m = ring8(first + step * i)
            shape = (2, rows.stop - rows.start)
            left = ref[m, :, rows].reshape(shape[0] * shape[1], 512)
            into[:, rows] += dot(left, weights(m, cols)).reshape(*shape, -1)
            return carry

        lax.fori_loop(0, count, body, 0)

    def forward_xn(*which_chunks):
        ring_xn.settle()
        forward(xn, aq, qkv_cols, slice(0, 256), *which_chunks)

    def group(half):
        return slice(half * 128, half * 128 + 128)

    def forward_dy(half, *which_chunks):
        ring_dy.settle(half)
        forward(dy, aa, out_cols, group(half), *which_chunks)

    forward_xn(-1, 1, 3)
    ring_xn.take(4, then=(6,))
    ring_dy.send(5, 6)
    forward_dy(0, -1, 1, 3)
    ring_xn.take(5)
    ring_xn.share(4, 5)
    forward_xn(-2, 4, 2)
    ring_dy.take(4)
    ring_dy.hand(dy.at[ring8(4), core, pl.ds(0, 128)])
    forward_dy(0, -2, 4, 2)
    forward_dy(0, -3, 6, 2)
    forward_xn(-3, 6, 2)
    ring_xn.take(6)
    ring_xn.hand(xn.at[ring8(4), core])
    forward_dy(0, 4, 0, 1)

    def strip(at):
        return pl.ds(pl.multiple_of(at * 16, 16), 16)

    def swap_out(arrays, parts):
        trips = copy.batch()
        for k in range(1, 8):
            src = sb.at[arrays, parts, :, strip(lax.rem(tm + k, 8))]
            trips(src, rb.at[arrays, parts, :, tm], along_tm(k))
        rb[arrays, parts, :, tm] = sb[arrays, parts, :, strip(tm), :]
        return trips

    def swap_back(arrays, parts):
        trips = copy.batch()
        for k in range(1, 8):
            dst = gb.at[arrays, parts, :, strip(tm)]
            trips(ob.at[arrays, parts, :, lax.rem(tm + k, 8)], dst, along_tm(k))
        gb[arrays, parts, :, strip(tm), :] = ob[arrays, parts, :, tm]
        return trips

    both = pl.ds(0, 2)
    one = (pl.ds(0, 1), pl.ds(1, 1))

    def grads_out(part):
        for s in range(2):
            sb[3, part, s] = aa[s, group(part)].astype(BF)
        return swap_out(pl.ds(3, 1), one[part])

    away = [grads_out(0)]
    forward_xn(4, 0, 1)
    for s in range(2):
        for a in range(3):
            for part in range(2):
                sb[a, part, s] = aq[s, group(part), a * HS : (a + 1) * HS].astype(BF)
    trips = swap_out(pl.ds(0, 3), both)
    ring_dy.take(5, then=(7,))
    ring_dy.take(6, then=(8,))
    ring_dy.share(5, 6, half=1)
    forward_dy(1, -1, 1, 3)
    ring_dy.take(7, then=(9,))
    forward_dy(1, -2, 4, 2)
    ring_dy.take(8)
    ring_dy.share(7, 8, half=1)
    forward_dy(1, -3, 6, 2)
    ring_dy.take(9)
    ring_dy.hand(dy.at[ring8(4), core, pl.ds(128, 128)], 1)
    trips.wait()

    row_id = lax.broadcasted_iota(jnp.int32, (256, 256), 0)
    col_id = lax.broadcasted_iota(jnp.int32, (256, 256), 1)
    same = ((row_id & 15) == (col_id & 15)) & ((row_id >> 7) == (col_id >> 7))
    seen = same & ((row_id >> 4) >= (col_id >> 4))
    scale = HS ** (-0.5)

    def held(i, part):
        return rb[i, part].reshape(256, HS)

    def attend(part):
        q, k, v = (held(i, part) for i in range(3))
        scores = jnp.where(seen, dot_t(q, k) * scale, -1e30)
        expo = jnp.exp(scores - jnp.max(scores, axis=1, keepdims=True))
        soft = expo / jnp.sum(expo, axis=1, keepdims=True)
        so[part] = soft
        st[part] = soft.T.astype(BF)
        ob[0, part] = dot(soft.astype(BF), v).astype(BF).reshape(2, 8, 16, HS)

    def attend_back(part):
        away[part].wait()
        q, k, v, a = (held(i, part) for i in range(4))
        soft = so[part]
        dsoft = dot_t(a, v)
        dscore = soft * (dsoft - jnp.sum(dsoft * soft, axis=1, keepdims=True)) * scale
        results = (
            dot(dscore.astype(BF), k),
            dot(dscore.T.astype(BF), q),
            dot(st[part], a),
        )
        for i, value in enumerate(results):
            ob[1 + i, part] = value.astype(BF).reshape(2, 8, 16, HS)
        return swap_back(pl.ds(1, 3), one[part])

    attend(0)
    attend(1)
    forward_dy(1, 4, 0, 1)
    away.append(grads_out(1))
    att_trips = swap_back(pl.ds(0, 1), both)
    back = [attend_back(0)]
    back.append(attend_back(1))

    def keep_transposed(a, parts=(0, 1)):
        for part in parts:
            for s in range(2):
                first = s * 256 + part * 128
                source = gb[(a + 1) % 4, part, s].astype(F32)
                gt[a * HS : (a + 1) * HS, first : first + 128] = source.T.astype(BF)

    def out_grad(m, carry):
        value = dot(gt[3 * HS :, :], dy[m].reshape(512, 512)).astype(BF)
        place = wt_o.at[lax.div(m, 4), lo(hi(m)), lo(m)]
        for i in range(4):
            place[i // 2, i % 2] = value[:, i * HS : (i + 1) * HS]
        return carry


    offsets = (4, 3, -3, 2, -2, 1, -1, 0)

    def grads_in(half):
        for s in range(2):
            for a in range(3):
                gc[s, group(half), a * HS : (a + 1) * HS] = gb[1 + a, half, s]

    needs = (((0, 2), (1, 4), (3, 6), (5, 7)), ((0, 1), (3, 2), (5, 4), (6, 7)))

    def input_grads(half, order):
        met = copy.batch()
        rows = group(half)
        for index in needs[half][order]:
            w = weights(ring8(offsets[index]), qkv_cols)
            value = dot_t(gc[:, rows, :].reshape(256, 3 * HS), w).astype(BF)
            ps[index, :, rows, :] = value.reshape(2, 128, 512)
            part = pl.ds(half * 128, 128)
            met(ps.at[index, other, part], sr.at[index, part], sibling)
        across[half, order] = met

    across = {}

    def total_of(index, rows):
        return ps[index, core, rows, :].astype(F32) + sr[index, rows, :].astype(F32)

    ways = (((4, 3, 2, 1), (3, 2, 1)), ((3, 2, 1), (4, 3, 2, 1)))
    flying = {}

    def hop(half, order):
        across.pop((half, order)).wait()
        slot = half * 4 + order
        for quarter in range(2):
            if order:
                flying[half, quarter].wait()
            trip = copy.batch()
            flying[half, quarter] = trip
            part = slice(quarter * 64, quarter * 64 + 64)
            rows = slice(half * 128 + part.start, half * 128 + part.stop)
            for d in range(2):
                way = ways[half][d]
                if order >= len(way):
                    continue
                distance = way[order]
                offset = 4 if distance == 4 else (distance, -distance)[d]
                value = total_of(offsets.index(offset), rows)
                if order:
                    value = value + cr[d, slot - 1, part, :].astype(F32)
                cs[d, slot, part, :] = value.astype(BF)
                place = (d, slot, pl.ds(part.start, 64))
                trip(cs.at[place], cr.at[place], (zr, zl)[d])

    class Reduce:
        def __init__(self, part, right, left, got, tmp, end=None):
            self.part = part
            self.to = (right, left)
            self.got = got
            self.tmp = tmp
            self.ends, self.slots, self.second = end or (self.to, got, None)

        def far(self):
            self.first = copy.batch()
            self.first(self.part(2, 0), self.got.at[0], self.to[0])
            self.first(self.part(2, 1), self.got.at[1], self.to[1])

        def near(self):
            if self.second is None:
                self.second = copy.batch()
            self.second(self.part(1, 1), self.slots.at[2], self.ends[0])
            self.second(self.part(3, 0), self.slots.at[3], self.ends[1])

        def chain(self):
            self.first.wait()
            for d, (at, half) in enumerate(((1, 0), (3, 1))):
                value = self.part(at, half)[...].astype(F32) + self.got[d].astype(F32)
                self.tmp[d] = value.astype(BF)
                self.second(self.tmp.at[d], self.slots.at[4 + d], self.ends[d])

        def finish(self):
            self.second.wait()
            return joined(self.part(0, 0)[...], self.part(0, 1)[...], self.slots)

    def joined(first, second, got):
        return (
            first.astype(F32) + got[3].astype(F32) + got[4].astype(F32),
            second.astype(F32) + got[2].astype(F32) + got[5].astype(F32),
        )

    ending = copy.batch()

    def end_of(axis, slots):
        if axis == 0:
            ends = device_of(xs[1], y, axis), device_of(xs[3], y, axis)
        else:
            ends = device_of(x, ys[1], axis), device_of(x, ys[3], axis)
        return ends, slots.at[core], ending

    def out_first(axis):
        def part_a(j, half):
            return wt_o.at[hi(ys[j]), 0, half, :, lo(ys[j])]

        def part_b(j, half):
            return wt_o.at[half, 1, hi(xs[j]), lo(xs[j]), :]

        part, right, left = ((part_a, yr, yd), (part_b, xr, xl))[axis]
        return Reduce(part, right, left, ra_o.at[axis], ta_o.at[axis])

    def out_second(axis):
        ring = (xs, ys)[axis]

        def part(j, half):
            return r1_o.at[axis, hi(ring[j]), lo(ring[j]), pl.ds(half * 64, 64)]

        right, left = ((xr, xl), (yr, yd))[axis]
        end = end_of(axis, re_o)
        return Reduce(part, right, left, rc_o.at[axis], tc_o.at[axis], end)

    out1 = [out_first(axis) for axis in range(2)]
    out2 = [out_second(axis) for axis in range(2)]
    att_trips.wait()
    keep_transposed(3)
    lax.fori_loop(0, 8, out_grad, 0)
    for stage in out1:
        stage.far()
        stage.near()
    back[0].wait()
    grads_in(0)
    input_grads(0, 0)
    for a in range(3):
        keep_transposed(a, (0,))
    hop(0, 0)
    input_grads(0, 1)
    back[1].wait()
    grads_in(1)
    input_grads(1, 0)

    for a in range(3):
        keep_transposed(a, (1,))

    def weight_grad(yh_at, s_at, xh_at):
        m = (yh_at * 2 + s_at) * 2 + xh_at
        value = dot(gt[: 3 * HS, :], xn[m].reshape(512, 512)).astype(BF)
        for i in range(4):
            wt[yh_at, s_at, xh_at, i // 2, i % 2] = value[:, i * HS : (i + 1) * HS]

    def grads(which_chunk):
        def body(i, carry):
            weight_grad(*which_chunk(i))
            return carry

        lax.fori_loop(0, 2, body, 0)

    def half_rows(half):
        return slice(half * 192, half * 192 + 192)

    def first_stage(axis, k):
        def part_a(j, half):
            at = ys[j]
            return wt.at[hi(at), 0, hi(xs[k]), lo(xs[k]), lo(at), half_rows(half)]

        def part_b(j, half):
            at = xs[j]
            return wt.at[hi(ys[k]), 1, hi(at), lo(at), lo(ys[k]), half_rows(half)]

        part, right, left = ((part_a, yr, yd), (part_b, xr, xl))[axis]
        return Reduce(part, right, left, ra.at[axis, k], ta.at[axis, k])

    def second_stage(axis):
        def part(j, half):
            return r1.at[axis, j, half_rows(half)]

        right, left = ((xr, xl), (yr, yd))[axis]
        end = end_of(axis, re)
        return Reduce(part, right, left, rc.at[axis], tc.at[axis], end)

    stage1 = [[first_stage(axis, k) for k in range(4)] for axis in range(2)]
    stage2 = [second_stage(axis) for axis in range(2)]

    def chain(k):
        for axis in range(2):
            stage1[axis][k].chain()

    def finish(k):
        for axis in range(2):
            for half, value in enumerate(stage1[axis][k].finish()):
                r1[axis, k, half_rows(half), :] = value.astype(BF)

    def start(axis, *groups):
        for k in groups:
            stage1[axis][k].far()
            stage1[axis][k].near()

    weight_grad(1 - yh, 0, 1 - xh)
    stage1[0][2].far()
    weight_grad(yh, 0, 1 - xh)
    stage1[0][2].near()
    hop(1, 0)
    weight_grad(1 - yh, 1, 1 - xh)
    stage1[1][2].far()
    weight_grad(1 - yh, 1, xh)
    stage1[1][2].near()
    grads(lambda i: (i, 0, xh))
    start(0, 1, 3, 0)
    hop(0, 1)
    grads(lambda i: (yh, 1, i))
    start(1, 1, 3, 0)
    input_grads(1, 1)
    chain(2)
    for stage in out1:
        stage.chain()
    input_grads(0, 2)
    hop(1, 1)
    hop(0, 2)
    input_grads(1, 2)

    for s in range(2):
        prod = jnp.zeros((256, HS), F32)
        for a in range(3):
            left = jnp.concatenate([gb[1 + a, part, s] for part in range(2)], axis=0)
            right = jnp.concatenate([sb[a, part, s] for part in range(2)], axis=0)
            prod = prod + left.astype(F32) * right.astype(F32)
        ts[s] = jnp.broadcast_to(jnp.sum(prod.T, axis=0, keepdims=True), (8, 256))
    inner_pair = copy(ts.at[other], tr, sibling)

    chain(1)
    hop(1, 2)
    chain(3)
    finish(2)
    for axis in range(2):
        stage2[axis].far()
    input_grads(0, 3)
    input_grads(1, 3)
    chain(0)
    hop(0, 3)
    for axis in range(2):
        for half, value in enumerate(out1[axis].finish()):
            r1_o[axis, half] = value.astype(BF)
        out2[axis].far()
        out2[axis].near()
    inner_pair.wait()
    tl[...] = ts[core] + tr[...]
    tt[mp] = tl[...]
    inner = copy.batch()
    for k in range(1, 8):
        inner(tl, tt.at[mp], along_z(k))
    finish(1)
    finish(3)
    for axis in range(2):
        stage2[axis].near()
    hop(1, 3)
    for stage in out2:
        stage.chain()
    finish(0)
    for axis in range(2):
        stage2[axis].chain()

    def out_place(axis):
        return r1_o.at[axis, xh + axis * (yh - xh), lo(x) + axis * (yl - lo(x))]

    ending(r1.at[other, 0], oc.at[core], sibling)
    ending(out_place(other), oc_o.at[core], sibling)
    oc[core] = r1[core, 0]
    oc_o[core] = out_place(core)[...]

    inner.wait()
    inner_row = tt[0]
    for k in range(1, 8):
        inner_row = inner_row + tt[k]
    inner_col = jnp.broadcast_to(inner_row[0:1, :] / 4096.0, (HS, 256)).T
    for half in range(2):
        rows = group(half)
        for quarter in range(2):
            flying[half, quarter].wait()
        grad = total_of(7, rows)
        for d in range(2):
            final = len(ways[half][d]) - 1
            grad = grad + cr[d, half * 4 + final].astype(F32)
        inverse = iv[rows, :]
        back = inverse * inverse * inner_col[rows, :]
        for g in range(4):
            cols = slice(g * HS, (g + 1) * HS)
            scaled = grad[:, cols] * gain[:, cols]
            branch = inverse * scaled - xs_in[rows, cols].astype(F32) * back
            value = (dy[mp, core, rows, cols].astype(F32) + branch).astype(BF)
            for j in range(2):
                span_v[j, rows, cols] = jnp.where(which == j, value, jnp.zeros_like(value))
    written = [fetch(span_v, span_out.at[0])]

    ending.wait()
    for h in range(2):
        cols = slice(h * HS, (h + 1) * HS)
        halves_of = joined(oc[h, :192, :], oc[h, 192:, :], re.at[h])
        whole = jnp.concatenate(halves_of, axis=0)
        for a in range(3):
            g_v[a, :, cols] = whole[a * HS : (a + 1) * HS, :].T
        first, second = joined(oc_o[h, :64, :], oc_o[h, 64:, :], re_o.at[h])
        o_v[h * HS : h * HS + 64, :] = first
        o_v[h * HS + 64 : (h + 1) * HS, :] = second
    for a, ref in enumerate((q_out, k_out, v_out)):
        written.append(fetch(g_v.at[a], ref))
    written.append(fetch(o_v, o_out))
    copy.finish()
    for c in written:
        c.wait()


def hand_over(*refs):
    ins, outs, held, sems = refs[:5], refs[5:10], refs[10:15], refs[15]
    fetched = [pltpu.make_async_copy(ins[i], held[i], sems.at[0, i]) for i in range(5)]
    written = [pltpu.make_async_copy(held[i], outs[i], sems.at[1, i]) for i in range(5)]
    for c in fetched:
        c.start()
    for i in range(5):
        fetched[i].wait()
        written[i].start()
    for c in written:
        c.wait()


def local(spans, frame_span, norm_gain, w_query, w_key, w_value, w_out, grad_out):
    vmem = pl.BlockSpec(memory_space=pltpu.VMEM)
    smem = pl.BlockSpec(memory_space=pltpu.SMEM)
    anywhere = pl.BlockSpec(memory_space=pl.ANY)
    shape = jax.ShapeDtypeStruct
    scratch = [
        ((2, 256, 512), BF),
        ((256, 512), BF),
        ((8, 2, 256, 512), BF),
        ((8, 2, 256, 512), BF),
        ((3, 128, 256), BF),
        ((256, 128), BF),
        ((2, 128, 512), BF),
        ((2, 2, 2, 2, 2, 128, 512), BF),
        ((8, 8, 256), F32),
        ((8, 256), F32),
        ((256, 128), F32),
        ((2, 256, 384), F32),
        ((2, 256, 128), F32),
        ((4, 2, 2, 128, 128), BF),
        ((4, 2, 2, 8, 16, 128), BF),
        ((2, 256, 256), F32),
        ((2, 256, 256), BF),
        ((4, 2, 2, 8, 16, 128), BF),
        ((4, 2, 2, 128, 128), BF),
        ((2, 256, 384), BF),
        ((512, 512), BF),
        ((2, 8, 256), F32),
        ((8, 256), F32),
        ((8, 256), F32),
        ((8, 8, 256), F32),
        ((8, 2, 256, 512), BF),
        ((8, 256, 512), BF),
        ((2, 8, 128, 512), BF),
        ((2, 8, 128, 512), BF),
        ((2, 2, 2, 2, 2, 384, 128), BF),
        ((2, 2, 2, 2, 2, 128, 128), BF),
        ((2, 6, 2, 128, 128), BF),
        ((2, 2, 2, 128, 128), BF),
        ((2, 2, 2, 128, 128), BF),
        ((2, 6, 64, 128), BF),
        ((2, 2, 64, 128), BF),
        ((2, 4, 6, 192, 128), BF),
        ((2, 4, 2, 192, 128), BF),
        ((2, 4, 384, 128), BF),
        ((2, 6, 192, 128), BF),
        ((2, 2, 192, 128), BF),
        ((2, 6, 192, 128), BF),
        ((2, 6, 64, 128), BF),
        ((2, 384, 128), BF),
        ((2, 128, 128), BF),
        ((2, 256, 512), BF),
        ((3, 128, 256), F32),
        ((256, 128), F32),
        ((RULER, 256), F32),
    ]
    out_shape = (
        shape((1, 2, 256, 512), BF),
        shape((128, 256), F32),
        shape((128, 256), F32),
        shape((128, 256), F32),
        shape((256, 128), F32),
    )
    results = pl.pallas_call(
        kernel,
        out_shape=out_shape,
        in_specs=[anywhere, smem, vmem] + [anywhere] * 5,
        out_specs=(anywhere,) * 5,
        scratch_shapes=[pltpu.VMEM(*each) for each in scratch]
        + [pltpu.SemaphoreType.DMA((n,)) for n in (DEPARTURES, ARRIVALS, 11)],
        compiler_params=pltpu.CompilerParams(
            collective_id=0, has_side_effects=True, vmem_limit_bytes=56 * 1024 * 1024
        ),
    )(spans, frame_span, norm_gain, w_query, w_key, w_value, w_out, grad_out)
    return pl.pallas_call(
        hand_over,
        out_shape=out_shape,
        in_specs=[anywhere] * 5,
        out_specs=(anywhere,) * 5,
        scratch_shapes=[pltpu.VMEM(each.shape, each.dtype) for each in out_shape]
        + [pltpu.SemaphoreType.DMA((2, 5))],
    )(*results)


def solution(mesh):
    placed = (
        P("dp", "tm", None, "mp"),
        P("dp", "tm"),
        P("mp"),
        P(("dp", "tm"), "mp"),
        P(("dp", "tm"), "mp"),
        P(("dp", "tm"), "mp"),
        P("mp", ("dp", "tm")),
        P("dp", "tm", None, "mp"),
    )
    return jax.shard_map(
        local,
        mesh=mesh,
        in_specs=placed,
        out_specs=(
            P("dp", "tm", None, "mp"),
            P(("dp", "tm"), "mp"),
            P(("dp", "tm"), "mp"),
            P(("dp", "tm"), "mp"),
            P("mp", ("dp", "tm")),
        ),
        check_vma=False,
    )
```

```python
import math

import jax
import jax.numpy as jnp
from jax import lax
from jax.experimental import pallas as pl
from jax.experimental.pallas import tpu as pltpu
from jax.sharding import PartitionSpec as P

HS = 128
EPSILON = 1e-05
BF = jnp.bfloat16
F32 = jnp.float32
MESH = pl.DeviceIdType.MESH
ARRIVALS = 104
DEPARTURES = 4
RULER = 6144

ROWS_COLS = (((1,), (1,)), ((), ()))


def dot(left, right):
    return jnp.dot(left, right, preferred_element_type=F32)


def dot_t(left, right):
    return lax.dot_general(left, right, ROWS_COLS, preferred_element_type=F32)


class Batch:
    def __init__(self, copies, at):
        self.copies = copies
        self.at = at
        self.kib = 0

    def __call__(self, src, dst, device):
        copies = self.copies
        kib = math.prod(dst.shape) * jnp.dtype(dst.dtype).itemsize // 1024
        if copies.departed[-1] + kib > RULER:
            copies.departed.append(0)
        copies.departed[-1] += kib
        self.kib += kib
        pltpu.make_async_remote_copy(
            src_ref=src,
            dst_ref=dst,
            send_sem=copies.send.at[len(copies.departed) - 1],
            recv_sem=copies.recv.at[self.at],
            device_id=device,
            device_id_type=MESH,
        ).start()

    def wait(self):
        copies = self.copies
        copies.open.remove(self)
        copies.wait(copies.recv.at[self.at], self.kib)


class Copies:
    def __init__(self, send, recv, ruler):
        self.send = send
        self.recv = recv
        self.ruler = ruler
        self.departed = [0]
        self.count = 0
        self.open = []

    def batch(self):
        assert self.count < ARRIVALS
        new = Batch(self, self.count)
        self.count += 1
        self.open.append(new)
        return new

    def __call__(self, src, dst, device):
        new = self.batch()
        new(src, dst, device)
        return new

    def wait(self, sem, kib):
        span = self.ruler.at[pl.ds(0, kib)]
        pltpu.make_async_copy(span, span, sem).wait()

    def finish(self):
        assert not self.open
        assert len(self.departed) <= DEPARTURES
        for at, kib in enumerate(self.departed):
            self.wait(self.send.at[at], kib)


def kernel(
    spans_ref,
    which_ref,
    gain_ref,
    wq_ref,
    wk_ref,
    wv_ref,
    wo_ref,
    dy_ref,
    span_out,
    q_out,
    k_out,
    v_out,
    o_out,
    sp,
    xs_in,
    xn,
    dy,
    wl,
    wol,
    wp,
    wg,
    ss,
    sl,
    iv,
    aq,
    aa,
    sb,
    rb,
    so,
    st,
    ob,
    gb,
    gc,
    gt,
    ts,
    tr,
    tl,
    tt,
    ps,
    sr,
    cs,
    cr,
    wt,
    wt_o,
    ra_o,
    ta_o,
    r1_o,
    rc_o,
    tc_o,
    ra,
    ta,
    r1,
    rc,
    tc,
    re,
    re_o,
    oc,
    oc_o,
    span_v,
    g_v,
    o_v,
    ruler,
    send,
    recv,
    near_sem,
):
    dp = lax.axis_index("dp")
    tm = lax.axis_index("tm")
    mp = lax.axis_index("mp")
    core = lax.rem(dp, 2)
    other = 1 - core
    yh = lax.div(dp, 2)
    x = lax.div(tm, 2)
    yl = lax.rem(tm, 2)
    y = yh * 2 + yl

    def hi(v):
        return lax.div(v, 2)

    def lo(v):
        return lax.rem(v, 2)

    def device(x_at, y_at):
        return (hi(y_at) * 2 + core, x_at * 2 + lo(y_at), mp)

    def device_of(x_at, y_at, core_at):
        return (hi(y_at) * 2 + core_at, x_at * 2 + lo(y_at), mp)

    def ring8(offset):
        return lax.rem(mp + offset + 8, 8)

    def along_z(offset):
        return (dp, tm, ring8(offset))

    def along_tm(offset):
        return (dp, lax.rem(tm + offset, 8), mp)

    sibling = (yh * 2 + other, tm, mp)
    zr, zl = along_z(1), along_z(-1)
    xs = tuple(lax.rem(x + k, 4) for k in range(4))
    ys = tuple(lax.rem(y + k, 4) for k in range(4))
    xh = hi(x)
    xr, xl = device(xs[1], y), device(xs[3], y)
    yr, yd = device(x, ys[1]), device(x, ys[3])
    far_y = device(x, lax.rem(y + 3 + 2 * yl, 4))

    barrier = pltpu.get_barrier_semaphore()
    partners = [sibling, far_y]
    partners += [along_z(k) for k in range(1, 8)]
    partners += [along_tm(k) for k in range(1, 8)]
    partners += [device_of(xs[k], y, other) for k in (1, 3)]
    partners += [device_of(x, ys[k], other) for k in (1, 3)]
    for partner in partners:
        pl.semaphore_signal(barrier, inc=1, device_id=partner, device_id_type=MESH)

    fetched = []

    def fetch(src, dst):
        c = pltpu.make_async_copy(src, dst, near_sem.at[len(fetched)])
        c.start()
        fetched.append(c)
        return c

    span_in = fetch(spans_ref.at[0], sp)
    w_in = [fetch(ref, wl.at[a]) for a, ref in enumerate((wq_ref, wk_ref, wv_ref))]
    w_in.append(fetch(wo_ref, wol))
    dy_in = fetch(dy_ref.at[0, 0], dy.at[mp, core])

    which = which_ref[0, 0]
    gain = gain_ref[...].astype(F32).reshape(1, 512)
    span_in.wait()
    xs_in[...] = jnp.where(which == 0, sp[0], sp[1])
    sums = jnp.zeros((256, HS), F32)
    for g in range(4):
        part = xs_in[:, g * HS : (g + 1) * HS].astype(F32)
        sums = sums + part * part
    row = jnp.sum(sums.T, axis=0, keepdims=True)
    sl[...] = jnp.broadcast_to(row, (8, 256))
    for c in w_in:
        c.wait()
    for h in range(2):
        for a in range(3):
            wp[h, :, a * HS : (a + 1) * HS] = wl[a, :, h * HS : (h + 1) * HS]
        wp[h, :, 3 * HS :] = wol[h * HS : (h + 1) * HS, :].astype(F32).T.astype(BF)
    pl.semaphore_wait(barrier, len(partners))

    copy = Copies(send, recv, ruler)

    halves = (
        ((1, 0, 128), (1, 128, 128), (2, 0, 128), (2, 128, 128), (3, 0, 128), (3, 128, 128), (4, 0, 128)),
        ((1, 128, 128), (1, 0, 128), (2, 128, 128), (2, 0, 128), (3, 128, 128), (3, 0, 128), (4, 128, 128)),
    )
    first_half = ((1, 0, 128), (1, 128, 128), (2, 0, 128), (3, 0, 128))
    staged = (
        first_half
        + ((4, 0, 64), (2, 128, 64), (2, 192, 64))
        + ((3, 128, 64), (3, 192, 64), (4, 128, 64)),
        first_half
        + ((4, 64, 64), (2, 192, 64), (2, 128, 64))
        + ((3, 192, 64), (3, 128, 64), (4, 192, 64)),
    )

    class Ring:
        def __init__(self, ref, ways, src):
            self.ref = ref
            self.ways = ways
            self.src = src
            self.flight = {}
            self.pending = {}

        def part(self, d, k, first, rows):
            offset = -k if d == 0 else k
            return self.ref.at[ring8(offset), core, pl.ds(first, rows)]

        def pass_on(self, d, j):
            k, first, rows = self.ways[d][j]
            part = self.part(d, k - 1, first, rows)
            src = self.src.at[pl.ds(first, rows)] if k == 1 else part
            if d == 0:
                self.flight[j] = copy.batch()
            self.flight[j](src, part, (zr, zl)[d])

        def send(self, *which_parts):
            for j in which_parts:
                for d in range(2):
                    self.pass_on(d, j)

        def take(self, *which_parts, then=()):
            for at, j in enumerate(which_parts):
                self.flight[j].wait()
                if then:
                    self.send(then[at])

        def share(self, *which_parts, half=0):
            for d in range(2):
                rows = [self.ways[d][j] for j in which_parts]
                first = min(r[1] for r in rows)
                part = self.part(d, rows[0][0], first, sum(r[2] for r in rows))
                self.hand(part, half)

        def hand(self, part, half=0):
            if half not in self.pending:
                self.pending[half] = copy.batch()
            self.pending[half](part, part, sibling)

        def settle(self, half=0):
            if half in self.pending:
                self.pending.pop(half).wait()

    grad_in = dy_ref.at[0, 0]
    ring_dy = Ring(dy, staged, grad_in)
    sumsq = copy.batch()
    for k in range(1, 8):
        sumsq(sl, ss.at[mp], along_z(k))
    ss[mp] = sl[...]
    mine = wg.at[yh, core, xh, lo(x), yl]
    pair = copy(wp.at[other], mine, sibling)
    ring_dy.send(0, 1)
    wg[yh, core, xh, lo(x), yl] = wp[core]

    class Spread:
        def __init__(self, at, ring, right, left):
            self.at = at
            self.ring = ring
            self.to = (right, left)
            own = at(ring[0])
            self.trip = copy.batch()
            self.trip(own, own, right)
            self.trip(own, own, left)

        def relay(self):
            self.trip.wait()
            self.trip = copy.batch()
            part = self.at(self.ring[3]).at[pl.ds(0, 64)]
            self.trip(part, part, self.to[0])
            part = self.at(self.ring[1]).at[pl.ds(64, 64)]
            self.trip(part, part, self.to[1])

        def done(self):
            self.trip.wait()

    def block(x_at, y_at, s):
        return wg.at[hi(y_at), s, hi(x_at), lo(x_at), lo(y_at)]

    def spread_a(k):
        return Spread(lambda v: block(xs[k], v, 0), ys, yr, yd)

    def spread_b(k):
        return Spread(lambda v: block(v, ys[k], 1), xs, xr, xl)

    pair.wait()
    a1 = Spread(lambda v: block(v, y, 0), xs, xr, xl)
    b1 = Spread(lambda v: block(x, v, 1), ys, yr, yd)
    second = {0: (spread_a(0), spread_b(0))}

    sumsq.wait()
    total = ss[0]
    for k in range(1, 8):
        total = total + ss[k]
    inv_row = lax.rsqrt(total / 4096.0 + EPSILON)
    iv[...] = jnp.broadcast_to(inv_row[0:1, :], (HS, 256)).T
    for g in range(4):
        cols = slice(g * HS, (g + 1) * HS)
        xn[mp, core, :, cols] = (
            xs_in[:, cols].astype(F32) * iv[...] * gain[:, cols]
        ).astype(BF)
    ring_xn = Ring(xn, halves, xn.at[mp, core])
    ring_xn.send(0, 1)
    ring_xn.hand(xn.at[mp, core])
    ring_dy.take(0, then=(2,))
    aq[...] = jnp.zeros_like(aq)
    aa[...] = jnp.zeros_like(aa)

    a1.relay()
    b1.relay()
    for k in (3, 1):
        second[k] = (spread_a(k), spread_b(k))

    def relay(k):
        second[k][0].relay()
        second[k][1].relay()

    relay(0)
    dy_in.wait()
    ring_dy.hand(dy.at[mp, core, pl.ds(0, 128)], 0)
    ring_dy.hand(dy.at[mp, core, pl.ds(128, 128)], 1)
    ring_dy.take(1)
    ring_dy.share(0)
    ring_dy.share(1, half=1)
    a1.done()
    b1.done()
    second[2] = (spread_a(2), spread_b(2))
    ring_xn.take(0, then=(2,))
    ring_xn.take(1, then=(3,))
    ring_xn.share(0, 1)
    relay(3)
    ring_dy.take(2, then=(3,))
    ring_dy.share(2)
    relay(1)
    ring_xn.take(2, then=(4,))
    relay(2)
    ring_xn.take(3, then=(5,))
    ring_xn.share(2, 3)
    ring_dy.take(3, then=(4,))
    ring_dy.share(3)
    for k in range(4):
        second[k][0].done()
        second[k][1].done()

    def weights(m, cols):
        return wg[lax.div(m, 4), lo(hi(m)), lo(m), :, :, :, cols].reshape(512, -1)

    qkv_cols = slice(0, 3 * HS)
    out_cols = slice(3 * HS, 4 * HS)

    def forward(ref, into, cols, rows, first, step, count):
        def body(i, carry):
            m = ring8(first + step * i)
            shape = (2, rows.stop - rows.start)
            left = ref[m, :, rows].reshape(shape[0] * shape[1], 512)
            into[:, rows] += dot(left, weights(m, cols)).reshape(*shape, -1)
            return carry

        lax.fori_loop(0, count, body, 0)

    def forward_xn(*which_chunks):
        ring_xn.settle()
        forward(xn, aq, qkv_cols, slice(0, 256), *which_chunks)

    def group(half):
        return slice(half * 128, half * 128 + 128)

    def forward_dy(half, *which_chunks):
        ring_dy.settle(half)
        forward(dy, aa, out_cols, group(half), *which_chunks)

    forward_xn(-1, 1, 3)
    ring_xn.take(4, then=(6,))
    ring_dy.send(5, 6)
    forward_dy(0, -1, 1, 3)
    ring_xn.take(5)
    ring_xn.share(4, 5)
    forward_xn(-2, 4, 2)
    ring_dy.take(4)
    ring_dy.hand(dy.at[ring8(4), core, pl.ds(0, 128)])
    forward_dy(0, -2, 4, 2)
    forward_dy(0, -3, 6, 2)
    forward_xn(-3, 6, 2)
    ring_xn.take(6)
    ring_xn.hand(xn.at[ring8(4), core])
    forward_dy(0, 4, 0, 1)

    def strip(at):
        return pl.ds(pl.multiple_of(at * 16, 16), 16)

    def swap_out(arrays, parts):
        trips = copy.batch()
        for k in range(1, 8):
            src = sb.at[arrays, parts, :, strip(lax.rem(tm + k, 8))]
            trips(src, rb.at[arrays, parts, :, tm], along_tm(k))
        rb[arrays, parts, :, tm] = sb[arrays, parts, :, strip(tm), :]
        return trips

    def swap_back(arrays, parts):
        trips = copy.batch()
        for k in range(1, 8):
            dst = gb.at[arrays, parts, :, strip(tm)]
            trips(ob.at[arrays, parts, :, lax.rem(tm + k, 8)], dst, along_tm(k))
        gb[arrays, parts, :, strip(tm), :] = ob[arrays, parts, :, tm]
        return trips

    both = pl.ds(0, 2)
    one = (pl.ds(0, 1), pl.ds(1, 1))

    def grads_out(part):
        for s in range(2):
            sb[3, part, s] = aa[s, group(part)].astype(BF)
        return swap_out(pl.ds(3, 1), one[part])

    away = [grads_out(0)]
    forward_xn(4, 0, 1)
    for s in range(2):
        for a in range(3):
            for part in range(2):
                sb[a, part, s] = aq[s, group(part), a * HS : (a + 1) * HS].astype(BF)
    trips = swap_out(pl.ds(0, 3), both)
    ring_dy.take(5, then=(7,))
    ring_dy.take(6, then=(8,))
    ring_dy.share(5, 6, half=1)
    forward_dy(1, -1, 1, 3)
    ring_dy.take(7, then=(9,))
    forward_dy(1, -2, 4, 2)
    ring_dy.take(8)
    ring_dy.share(7, 8, half=1)
    forward_dy(1, -3, 6, 2)
    ring_dy.take(9)
    ring_dy.hand(dy.at[ring8(4), core, pl.ds(128, 128)], 1)
    trips.wait()

    row_id = lax.broadcasted_iota(jnp.int32, (256, 256), 0)
    col_id = lax.broadcasted_iota(jnp.int32, (256, 256), 1)
    same = ((row_id & 15) == (col_id & 15)) & ((row_id >> 7) == (col_id >> 7))
    seen = same & ((row_id >> 4) >= (col_id >> 4))
    scale = HS ** (-0.5)

    def held(i, part):
        return rb[i, part].reshape(256, HS)

    def attend(part):
        q, k, v = (held(i, part) for i in range(3))
        scores = jnp.where(seen, dot_t(q, k) * scale, -1e30)
        expo = jnp.exp(scores - jnp.max(scores, axis=1, keepdims=True))
        soft = expo / jnp.sum(expo, axis=1, keepdims=True)
        so[part] = soft
        st[part] = soft.T.astype(BF)
        ob[0, part] = dot(soft.astype(BF), v).astype(BF).reshape(2, 8, 16, HS)

    def attend_back(part):
        away[part].wait()
        q, k, v, a = (held(i, part) for i in range(4))
        soft = so[part]
        dsoft = dot_t(a, v)
        dscore = soft * (dsoft - jnp.sum(dsoft * soft, axis=1, keepdims=True)) * scale
        results = (
            dot(dscore.astype(BF), k),
            dot(dscore.T.astype(BF), q),
            dot(st[part], a),
        )
        for i, value in enumerate(results):
            ob[1 + i, part] = value.astype(BF).reshape(2, 8, 16, HS)
        return swap_back(pl.ds(1, 3), one[part])

    attend(0)
    attend(1)
    forward_dy(1, 4, 0, 1)
    away.append(grads_out(1))
    att_trips = swap_back(pl.ds(0, 1), both)
    back = [attend_back(0)]
    back.append(attend_back(1))

    def keep_transposed(a, parts=(0, 1)):
        for part in parts:
            for s in range(2):
                first = s * 256 + part * 128
                source = gb[(a + 1) % 4, part, s].astype(F32)
                gt[a * HS : (a + 1) * HS, first : first + 128] = source.T.astype(BF)

    def out_grad(m, carry):
        value = dot(gt[3 * HS :, :], dy[m].reshape(512, 512)).astype(BF)
        place = wt_o.at[lax.div(m, 4), lo(hi(m)), lo(m)]
        for i in range(4):
            place[i // 2, i % 2] = value[:, i * HS : (i + 1) * HS]
        return carry


    offsets = (4, 3, -3, 2, -2, 1, -1, 0)

    def grads_in(half):
        for s in range(2):
            for a in range(3):
                gc[s, group(half), a * HS : (a + 1) * HS] = gb[1 + a, half, s]

    needs = (((0, 2), (1, 4), (3, 6), (5, 7)), ((0, 1), (3, 2), (5, 4), (6, 7)))

    def input_grads(half, order):
        met = copy.batch()
        rows = group(half)
        for index in needs[half][order]:
            w = weights(ring8(offsets[index]), qkv_cols)
            value = dot_t(gc[:, rows, :].reshape(256, 3 * HS), w).astype(BF)
            ps[index, :, rows, :] = value.reshape(2, 128, 512)
            part = pl.ds(half * 128, 128)
            met(ps.at[index, other, part], sr.at[index, part], sibling)
        across[half, order] = met

    across = {}

    def total_of(index, rows):
        return ps[index, core, rows, :].astype(F32) + sr[index, rows, :].astype(F32)

    ways = (((4, 3, 2, 1), (3, 2, 1)), ((3, 2, 1), (4, 3, 2, 1)))
    flying = {}

    def hop(half, order):
        across.pop((half, order)).wait()
        slot = half * 4 + order
        for quarter in range(2):
            if order:
                flying[half, quarter].wait()
            trip = copy.batch()
            flying[half, quarter] = trip
            part = slice(quarter * 64, quarter * 64 + 64)
            rows = slice(half * 128 + part.start, half * 128 + part.stop)
            for d in range(2):
                way = ways[half][d]
                if order >= len(way):
                    continue
                distance = way[order]
                offset = 4 if distance == 4 else (distance, -distance)[d]
                value = total_of(offsets.index(offset), rows)
                if order:
                    value = value + cr[d, slot - 1, part, :].astype(F32)
                cs[d, slot, part, :] = value.astype(BF)
                place = (d, slot, pl.ds(part.start, 64))
                trip(cs.at[place], cr.at[place], (zr, zl)[d])

    class Reduce:
        def __init__(self, part, right, left, got, tmp, end=None):
            self.part = part
            self.to = (right, left)
            self.got = got
            self.tmp = tmp
            self.ends, self.slots, self.second = end or (self.to, got, None)

        def far(self):
            self.first = copy.batch()
            self.first(self.part(2, 0), self.got.at[0], self.to[0])
            self.first(self.part(2, 1), self.got.at[1], self.to[1])

        def near(self):
            if self.second is None:
                self.second = copy.batch()
            self.second(self.part(1, 1), self.slots.at[2], self.ends[0])
            self.second(self.part(3, 0), self.slots.at[3], self.ends[1])

        def chain(self):
            self.first.wait()
            for d, (at, half) in enumerate(((1, 0), (3, 1))):
                value = self.part(at, half)[...].astype(F32) + self.got[d].astype(F32)
                self.tmp[d] = value.astype(BF)
                self.second(self.tmp.at[d], self.slots.at[4 + d], self.ends[d])

        def finish(self):
            self.second.wait()
            return joined(self.part(0, 0)[...], self.part(0, 1)[...], self.slots)

    def joined(first, second, got):
        return (
            first.astype(F32) + got[3].astype(F32) + got[4].astype(F32),
            second.astype(F32) + got[2].astype(F32) + got[5].astype(F32),
        )

    ending = copy.batch()

    def end_of(axis, slots):
        if axis == 0:
            ends = device_of(xs[1], y, axis), device_of(xs[3], y, axis)
        else:
            ends = device_of(x, ys[1], axis), device_of(x, ys[3], axis)
        return ends, slots.at[core], ending

    def out_first(axis):
        def part_a(j, half):
            return wt_o.at[hi(ys[j]), 0, half, :, lo(ys[j])]

        def part_b(j, half):
            return wt_o.at[half, 1, hi(xs[j]), lo(xs[j]), :]

        part, right, left = ((part_a, yr, yd), (part_b, xr, xl))[axis]
        return Reduce(part, right, left, ra_o.at[axis], ta_o.at[axis])

    def out_second(axis):
        ring = (xs, ys)[axis]

        def part(j, half):
            return r1_o.at[axis, hi(ring[j]), lo(ring[j]), pl.ds(half * 64, 64)]

        right, left = ((xr, xl), (yr, yd))[axis]
        end = end_of(axis, re_o)
        return Reduce(part, right, left, rc_o.at[axis], tc_o.at[axis], end)

    out1 = [out_first(axis) for axis in range(2)]
    out2 = [out_second(axis) for axis in range(2)]
    att_trips.wait()
    keep_transposed(3)
    lax.fori_loop(0, 8, out_grad, 0)
    for stage in out1:
        stage.far()
        stage.near()
    back[0].wait()
    grads_in(0)
    input_grads(0, 0)
    for a in range(3):
        keep_transposed(a, (0,))
    hop(0, 0)
    input_grads(0, 1)
    back[1].wait()
    grads_in(1)
    input_grads(1, 0)

    for a in range(3):
        keep_transposed(a, (1,))

    def weight_grad(yh_at, s_at, xh_at):
        m = (yh_at * 2 + s_at) * 2 + xh_at
        value = dot(gt[: 3 * HS, :], xn[m].reshape(512, 512)).astype(BF)
        for i in range(4):
            wt[yh_at, s_at, xh_at, i // 2, i % 2] = value[:, i * HS : (i + 1) * HS]

    def grads(which_chunk):
        def body(i, carry):
            weight_grad(*which_chunk(i))
            return carry

        lax.fori_loop(0, 2, body, 0)

    def half_rows(half):
        return slice(half * 192, half * 192 + 192)

    def first_stage(axis, k):
        def part_a(j, half):
            at = ys[j]
            return wt.at[hi(at), 0, hi(xs[k]), lo(xs[k]), lo(at), half_rows(half)]

        def part_b(j, half):
            at = xs[j]
            return wt.at[hi(ys[k]), 1, hi(at), lo(at), lo(ys[k]), half_rows(half)]

        part, right, left = ((part_a, yr, yd), (part_b, xr, xl))[axis]
        return Reduce(part, right, left, ra.at[axis, k], ta.at[axis, k])

    def second_stage(axis):
        def part(j, half):
            return r1.at[axis, j, half_rows(half)]

        right, left = ((xr, xl), (yr, yd))[axis]
        end = end_of(axis, re)
        return Reduce(part, right, left, rc.at[axis], tc.at[axis], end)

    stage1 = [[first_stage(axis, k) for k in range(4)] for axis in range(2)]
    stage2 = [second_stage(axis) for axis in range(2)]

    def chain(k):
        for axis in range(2):
            stage1[axis][k].chain()

    def finish(k):
        for axis in range(2):
            for half, value in enumerate(stage1[axis][k].finish()):
                r1[axis, k, half_rows(half), :] = value.astype(BF)

    def start(axis, *groups):
        for k in groups:
            stage1[axis][k].far()
            stage1[axis][k].near()

    weight_grad(1 - yh, 0, 1 - xh)
    stage1[0][2].far()
    weight_grad(yh, 0, 1 - xh)
    stage1[0][2].near()
    hop(1, 0)
    weight_grad(1 - yh, 1, 1 - xh)
    stage1[1][2].far()
    weight_grad(1 - yh, 1, xh)
    stage1[1][2].near()
    grads(lambda i: (i, 0, xh))
    start(0, 1, 3, 0)
    hop(0, 1)
    grads(lambda i: (yh, 1, i))
    start(1, 1, 3, 0)
    input_grads(1, 1)
    chain(2)
    for stage in out1:
        stage.chain()
    input_grads(0, 2)
    hop(1, 1)
    hop(0, 2)
    input_grads(1, 2)

    for s in range(2):
        prod = jnp.zeros((256, HS), F32)
        for a in range(3):
            left = jnp.concatenate([gb[1 + a, part, s] for part in range(2)], axis=0)
            right = jnp.concatenate([sb[a, part, s] for part in range(2)], axis=0)
            prod = prod + left.astype(F32) * right.astype(F32)
        ts[s] = jnp.broadcast_to(jnp.sum(prod.T, axis=0, keepdims=True), (8, 256))
    inner_pair = copy(ts.at[other], tr, sibling)

    chain(1)
    hop(1, 2)
    chain(3)
    finish(2)
    for axis in range(2):
        stage2[axis].far()
    input_grads(0, 3)
    input_grads(1, 3)
    chain(0)
    hop(0, 3)
    for axis in range(2):
        for half, value in enumerate(out1[axis].finish()):
            r1_o[axis, half] = value.astype(BF)
        out2[axis].far()
        out2[axis].near()
    inner_pair.wait()
    tl[...] = ts[core] + tr[...]
    tt[mp] = tl[...]
    inner = copy.batch()
    for k in range(1, 8):
        inner(tl, tt.at[mp], along_z(k))
    finish(1)
    finish(3)
    for axis in range(2):
        stage2[axis].near()
    hop(1, 3)
    for stage in out2:
        stage.chain()
    finish(0)
    for axis in range(2):
        stage2[axis].chain()

    def out_place(axis):
        return r1_o.at[axis, xh + axis * (yh - xh), lo(x) + axis * (yl - lo(x))]

    ending(r1.at[other, 0], oc.at[core], sibling)
    ending(out_place(other), oc_o.at[core], sibling)
    oc[core] = r1[core, 0]
    oc_o[core] = out_place(core)[...]

    inner.wait()
    inner_row = tt[0]
    for k in range(1, 8):
        inner_row = inner_row + tt[k]
    inner_col = jnp.broadcast_to(inner_row[0:1, :] / 4096.0, (HS, 256)).T
    for half in range(2):
        rows = group(half)
        for quarter in range(2):
            flying[half, quarter].wait()
        grad = total_of(7, rows)
        for d in range(2):
            final = len(ways[half][d]) - 1
            grad = grad + cr[d, half * 4 + final].astype(F32)
        inverse = iv[rows, :]
        back = inverse * inverse * inner_col[rows, :]
        for g in range(4):
            cols = slice(g * HS, (g + 1) * HS)
            scaled = grad[:, cols] * gain[:, cols]
            branch = inverse * scaled - xs_in[rows, cols].astype(F32) * back
            value = (dy[mp, core, rows, cols].astype(F32) + branch).astype(BF)
            for j in range(2):
                span_v[j, rows, cols] = jnp.where(which == j, value, jnp.zeros_like(value))
    written = [fetch(span_v, span_out.at[0])]

    ending.wait()
    for h in range(2):
        first, second = joined(oc_o[h, :64, :], oc_o[h, 64:, :], re_o.at[h])
        o_v[h * HS : h * HS + 64, :] = first
        o_v[h * HS + 64 : (h + 1) * HS, :] = second
    written.append(fetch(o_v, o_out))
    wholes = [
        jnp.concatenate(joined(oc[h, :192, :], oc[h, 192:, :], re.at[h]), axis=0) for h in range(2)
    ]
    for a, ref in enumerate((q_out, k_out, v_out)):
        for h in range(2):
            g_v[a, :, h * HS : (h + 1) * HS] = wholes[h][a * HS : (a + 1) * HS, :].T
        written.append(fetch(g_v.at[a], ref))
    copy.finish()
    for c in written:
        c.wait()


def hand_over(*refs):
    ins, outs, held, sems = refs[:5], refs[5:10], refs[10:15], refs[15]
    fetched = [pltpu.make_async_copy(ins[i], held[i], sems.at[0, i]) for i in range(5)]
    written = [pltpu.make_async_copy(held[i], outs[i], sems.at[1, i]) for i in range(5)]
    for c in fetched:
        c.start()
    for i in range(5):
        fetched[i].wait()
        written[i].start()
    for c in written:
        c.wait()


def local(spans, frame_span, norm_gain, w_query, w_key, w_value, w_out, grad_out):
    vmem = pl.BlockSpec(memory_space=pltpu.VMEM)
    smem = pl.BlockSpec(memory_space=pltpu.SMEM)
    anywhere = pl.BlockSpec(memory_space=pl.ANY)
    shape = jax.ShapeDtypeStruct
    scratch = [
        ((2, 256, 512), BF),
        ((256, 512), BF),
        ((8, 2, 256, 512), BF),
        ((8, 2, 256, 512), BF),
        ((3, 128, 256), BF),
        ((256, 128), BF),
        ((2, 128, 512), BF),
        ((2, 2, 2, 2, 2, 128, 512), BF),
        ((8, 8, 256), F32),
        ((8, 256), F32),
        ((256, 128), F32),
        ((2, 256, 384), F32),
        ((2, 256, 128), F32),
        ((4, 2, 2, 128, 128), BF),
        ((4, 2, 2, 8, 16, 128), BF),
        ((2, 256, 256), F32),
        ((2, 256, 256), BF),
        ((4, 2, 2, 8, 16, 128), BF),
        ((4, 2, 2, 128, 128), BF),
        ((2, 256, 384), BF),
        ((512, 512), BF),
        ((2, 8, 256), F32),
        ((8, 256), F32),
        ((8, 256), F32),
        ((8, 8, 256), F32),
        ((8, 2, 256, 512), BF),
        ((8, 256, 512), BF),
        ((2, 8, 128, 512), BF),
        ((2, 8, 128, 512), BF),
        ((2, 2, 2, 2, 2, 384, 128), BF),
        ((2, 2, 2, 2, 2, 128, 128), BF),
        ((2, 6, 2, 128, 128), BF),
        ((2, 2, 2, 128, 128), BF),
        ((2, 2, 2, 128, 128), BF),
        ((2, 6, 64, 128), BF),
        ((2, 2, 64, 128), BF),
        ((2, 4, 6, 192, 128), BF),
        ((2, 4, 2, 192, 128), BF),
        ((2, 4, 384, 128), BF),
        ((2, 6, 192, 128), BF),
        ((2, 2, 192, 128), BF),
        ((2, 6, 192, 128), BF),
        ((2, 6, 64, 128), BF),
        ((2, 384, 128), BF),
        ((2, 128, 128), BF),
        ((2, 256, 512), BF),
        ((3, 128, 256), F32),
        ((256, 128), F32),
        ((RULER, 256), F32),
    ]
    out_shape = (
        shape((1, 2, 256, 512), BF),
        shape((128, 256), F32),
        shape((128, 256), F32),
        shape((128, 256), F32),
        shape((256, 128), F32),
    )
    results = pl.pallas_call(
        kernel,
        out_shape=out_shape,
        in_specs=[anywhere, smem, vmem] + [anywhere] * 5,
        out_specs=(anywhere,) * 5,
        scratch_shapes=[pltpu.VMEM(*each) for each in scratch]
        + [pltpu.SemaphoreType.DMA((n,)) for n in (DEPARTURES, ARRIVALS, 11)],
        compiler_params=pltpu.CompilerParams(
            collective_id=0, has_side_effects=True, vmem_limit_bytes=56 * 1024 * 1024
        ),
    )(spans, frame_span, norm_gain, w_query, w_key, w_value, w_out, grad_out)
    return pl.pallas_call(
        hand_over,
        out_shape=out_shape,
        in_specs=[anywhere] * 5,
        out_specs=(anywhere,) * 5,
        scratch_shapes=[pltpu.VMEM(each.shape, each.dtype) for each in out_shape]
        + [pltpu.SemaphoreType.DMA((2, 5))],
    )(*results)


def solution(mesh):
    placed = (
        P("dp", "tm", None, "mp"),
        P("dp", "tm"),
        P("mp"),
        P(("dp", "tm"), "mp"),
        P(("dp", "tm"), "mp"),
        P(("dp", "tm"), "mp"),
        P("mp", ("dp", "tm")),
        P("dp", "tm", None, "mp"),
    )
    return jax.shard_map(
        local,
        mesh=mesh,
        in_specs=placed,
        out_specs=(
            P("dp", "tm", None, "mp"),
            P(("dp", "tm"), "mp"),
            P(("dp", "tm"), "mp"),
            P(("dp", "tm"), "mp"),
            P("mp", ("dp", "tm")),
        ),
        check_vma=False,
    )
```
